256 devices in a mesh: row: 16 (over y, z_hi), col: 16 (over z_lo, x, core).
Axes of the slice: x: 4, y: 4, z: 8 (z_hi: 4, z_lo: 2; z = z_hi * 2 + z_lo), core: 2. Of those that a mesh axis runs over, the one named last changes fastest.
Arguments:
- fields: float32 [2, 1024, 2048, 128], P(None, 'row', 'col'), may hold values from -6 to 6
- factor_one: float32 [1024, 32], P('row'), may hold values from -0.1875 to 0.1875
- factor_two: float32 [2048, 32], P('col'), may hold values from -0.125 to 0.125
- factor_three: float32 [128, 32], replicated, may hold values from -0.5 to 0.5
Outputs:
- core: float32 [2, 32, 32, 32], replicated
- gram_one: float32 [2, 1024, 1024], P(None, 'row', 'col')
- gram_two: float32 [2, 2048, 2048], P(None, 'col', 'row')
The draws below stay inside these ranges and needn't reach their ends.
All inputs are finite; a program needn't handle non-finite values.
Results may differ from the reference program's by a relative error of at most 0.000076.
Values sent between devices are 32-bit elements; how exact they have to be, the bound alone decides.
A program may use at most 64 MiB of HBM per device.

```python
import jax
import jax.numpy as jnp
from jax import lax

SPECIES = 2
K = 128
R = 32
I1 = 1024
I2 = 2048


def shard_levels(key, dims, cuts, least, top_value):
    factor_of = 1.0
    for axis_at, blocks in cuts:
        heights = jax.random.uniform(jax.random.fold_in(jax.random.fold_in(key, 6), axis_at), (blocks,), jnp.float32, least / len(cuts), top_value / len(cuts))
        factor_of = factor_of * jnp.repeat(jnp.exp(heights), dims[axis_at] // blocks).reshape((-1,) + (1,) * (len(dims) - 1 - axis_at))
    return factor_of


def centred(rng, shape, spread, most, shards=(), dtype=jnp.bfloat16):
    gain = shard_levels(rng, shape, shards, -0.22, 0.18) if shards else 1.0
    result = jax.random.normal(rng, shape, jnp.float32) * spread * gain
    return jnp.minimum(jnp.maximum(result, -most), most).astype(dtype)


def setup_inputs(seed: int = 0) -> dict:
    arg_keys = jax.random.split(jax.random.key(seed), 5)
    return {
        "fields": centred(arg_keys[0], (SPECIES, I1, I2, K), 1.0, 6.0, ((1, 16), (2, 16)), jnp.float32),
        "factor_one": centred(arg_keys[1], (I1, R), I1 ** -0.5, 0.1875, ((0, 16),), jnp.float32),
        "factor_two": centred(arg_keys[2], (I2, R), I2 ** -0.5, 0.125, ((0, 16),), jnp.float32),
        "factor_three": centred(arg_keys[3], (K, R), K ** -0.5, 0.5, (), jnp.float32),
    }


HIGH = lax.Precision.HIGHEST


def one_species(block, factor_one, factor_two, factor_three):
    projected_three = jnp.einsum('ijk,kt->ijt', block, factor_three, precision=HIGH)
    proj_one = jnp.einsum('ijt,jq->iqt', projected_three, factor_two, precision=HIGH)
    proj_two = jnp.einsum('ijt,ip->jpt', projected_three, factor_one, precision=HIGH)
    core = jnp.einsum('iqt,ip->pqt', proj_one, factor_one, precision=HIGH)
    flat_one = proj_one.reshape(I1, R * R)
    flat_two = proj_two.reshape(I2, R * R)
    gram_one = jnp.dot(flat_one, flat_one.T, precision=HIGH) / (R * R)
    gram_two = jnp.dot(flat_two, flat_two.T, precision=HIGH) / (R * R)
    return core, gram_one, gram_two


def reference(fields, factor_one, factor_two, factor_three):
    core, gram_one, gram_two = lax.map(lambda block: one_species(block, factor_one, factor_two, factor_three), fields)
    return core, gram_one, gram_two
```

```python
import functools

import jax
import jax.numpy as jnp
from jax import lax
from jax.experimental import pallas as pl
from jax.experimental.pallas import tpu as pltpu
from jax.sharding import PartitionSpec as P

F32 = jnp.float32
BF16 = jnp.bfloat16
MESH = pl.DeviceIdType.MESH
RANK = 32
CHUNKS = 8


def split(x):
    high = x.astype(BF16)
    return high, (x - high.astype(F32)).astype(BF16)


def dot(a, b, dims):
    return lax.dot_general(a, b, ((dims[0], dims[1]), ((), ())), preferred_element_type=F32)


def stack_factor(f):
    high, low = split(f.T)
    return jnp.concatenate([jnp.concatenate([high, high], 1), jnp.concatenate([low, low], 1)], 0)


def kernel(
    fields, f1, f2, f3, core_out, g1_out, g2_out,
    xbuf, p3, p2, p1, wcore,
    ry1, ryf, rz1, rzf, rc1, rx1, rxf, rl,
    p2c, p1t, p2r, p1r, cy, cz, cc,
    xsem, ss, rs,
):
    r, c = lax.axis_index("row"), lax.axis_index("col")
    y, h = r // 4, r % 4
    l, x, co = c // 8, (c // 2) % 4, c % 2

    def ring(v, d):
        return (v + d) % 4

    def at_y(d):
        return (ring(y, d) * 4 + h, c)

    def at_h(d):
        return (y * 4 + ring(h, d), c)

    def at_x(d):
        return (r, l * 8 + ring(x, d) * 2 + co)

    at_l = (r, (1 - l) * 8 + x * 2 + co)
    at_co = (r, l * 8 + x * 2 + (1 - co))
    at_t = (c, r)
    off_diagonal = r != c

    def load(i):
        s, q = i // 4, i % 4
        return pltpu.make_async_copy(fields.at[s, pl.ds(q * 16, 16)], xbuf.at[i], xsem.at[i])

    for i in range(CHUNKS):
        load(i).start()
    barrier = pltpu.get_barrier_semaphore()
    partners = [at(d) for at in (at_y, at_h, at_x) for d in (1, 2, 3)] + [at_l, at_co]
    for to in partners:
        pl.semaphore_signal(barrier, inc=1, device_id=to, device_id_type=MESH)

    @pl.when(off_diagonal)
    def _():
        pl.semaphore_signal(barrier, inc=1, device_id=at_t, device_id_type=MESH)

    sent = []

    def copy(idx, src, dst, to):
        return pltpu.make_async_remote_copy(
            src_ref=src, dst_ref=dst, send_sem=ss.at[idx], recv_sem=rs.at[idx], device_id=to, device_id_type=MESH
        )

    counter = [0]

    def new(n=1):
        counter[0] += n
        return counter[0] - n

    def send(idx, src, dst, to):
        copy(idx, src, dst, to).start()
        sent.append((idx, src))

    def arrived(idx, dst):
        copy(idx, dst, dst, at_co).wait_recv()

    l3 = stack_factor(f3[...])
    l1 = stack_factor(f1[...])
    l2 = stack_factor(f2[...])
    wcore[...] = jnp.zeros_like(wcore)
    for b in range(4):
        wcore[pl.ds(b * 64, 64), pl.ds(b * 32, 32)] = f1[...]

    for i in range(CHUNKS):
        load(i).wait()

        def pair(n, _, i=i):
            both = xbuf[i, pl.ds(n * 2, 2)].reshape(256, 128)
            high, low = split(both)
            out = dot(l3, jnp.concatenate([high, low], 1), ((1,), (1,)))
            out = out[:RANK] + out[RANK:]
            at = i * 16 + n * 2
            p3[pl.ds(pl.multiple_of(at * RANK, RANK), RANK), :] = out[:, :128]
            p3[pl.ds(pl.multiple_of(at * RANK + RANK, RANK), RANK), :] = out[:, 128:]
            return 0

        lax.fori_loop(0, 8, pair, 0, unroll=4)

    def slot_products(ys, hs):
        k = ys * 4 + hs
        halves = []
        for t2 in range(2):
            tile = p3[pl.ds(k + 16 * t2, 128, stride=RANK), :]
            halves.append(split(tile))
        right = [jnp.concatenate([jnp.concatenate([hi[s * 64:s * 64 + 64], lo[s * 64:s * 64 + 64]], 0) for s in range(2)], 1) for hi, lo in halves]
        out = dot(l1, jnp.concatenate(right, 1), ((1,), (0,)))
        out = out[:RANK] + out[RANK:]
        for t2 in range(2):
            for s in range(2):
                at = t2 * 256 + s * 128
                p2[ys, hs, s, pl.ds(t2 * RANK, RANK), :] = out[:, at:at + 128]
        right = jnp.concatenate([jnp.concatenate([hi, lo], 1) for hi, lo in halves], 0)
        out = dot(l2, right, ((1,), (1,)))
        out = out[:RANK] + out[RANK:]
        lk, xk, ck = k // 8, (k // 2) % 4, k % 2
        for t2 in range(2):
            p1[lk, xk, ck, pl.ds(t2 * RANK, RANK), :] = out[:, t2 * 128:t2 * 128 + 128]

    pl.semaphore_wait(barrier, len(partners) + jnp.where(off_diagonal, 1, 0))

    order = (2, 1, 3, 0)
    m_y1 = [new(4), new(4)]
    m_yf = {(side, s): new(4) for side in range(2) for s in range(2)}

    for dy in order:
        ys = ring(y, dy)
        for n, dh in enumerate(order):
            hs = ring(h, dh)
            slot_products(ys, hs)
            if dy == 2:
                send(m_y1[0] + n, p2.at[ys, hs, 0], ry1.at[0, hs], at_y(1))
                send(m_y1[1] + n, p2.at[ys, hs, 1], ry1.at[1, hs], at_y(3))
            elif dy == 1:
                send(m_yf[0, 1] + n, p2.at[ys, hs, 1], ryf.at[0, hs, 1], at_y(1))
            elif dy == 3:
                send(m_yf[1, 0] + n, p2.at[ys, hs, 0], ryf.at[1, hs, 0], at_y(3))

    m_core = new()
    send(m_core, p1.at[:, :, 1 - co], rc1, at_co)

    def y_late(n):
        hs = ring(h, order[n])
        arrived(m_y1[0] + n, ry1.at[0, hs])
        p2[ring(y, 1), hs, 0] += ry1[0, hs]
        send(m_yf[0, 0] + n, p2.at[ring(y, 1), hs, 0], ryf.at[0, hs, 0], at_y(1))
        arrived(m_y1[1] + n, ry1.at[1, hs])
        p2[ring(y, 3), hs, 1] += ry1[1, hs]
        send(m_yf[1, 1] + n, p2.at[ring(y, 3), hs, 1], ryf.at[1, hs, 1], at_y(3))

    for n in range(2):
        y_late(n)

    arrived(m_core, rc1)
    for lk in range(2):
        for xk in range(4):
            p1[lk, xk, co] += rc1[lk, xk]
    m_x1 = [new(), new()]
    m_xf = {(side, k): new() for side in range(2) for k in range(2)}
    send(m_x1[0], p1.at[0, ring(x, 2), co], rx1.at[0], at_x(1))
    send(m_x1[1], p1.at[1, ring(x, 2), co], rx1.at[1], at_x(3))
    send(m_xf[0, 1], p1.at[1, ring(x, 1), co], rxf.at[0, 1], at_x(1))
    send(m_xf[1, 0], p1.at[0, ring(x, 3), co], rxf.at[1, 0], at_x(3))

    for n in range(2, 4):
        y_late(n)

    def y_final(n):
        hs = ring(h, order[n])
        for s in (1, 0):
            for side in range(2):
                arrived(m_yf[side, s] + n, ryf.at[side, hs, s])
            p2[y, hs, s] += ryf[0, hs, s] + ryf[1, hs, s]

    m_z1 = [new(), new()]
    m_zf = {(side, s): new() for side in range(2) for s in range(2)}
    y_final(0)
    send(m_z1[0], p2.at[y, ring(h, 2), 0], rz1.at[0], at_h(1))
    send(m_z1[1], p2.at[y, ring(h, 2), 1], rz1.at[1], at_h(3))

    arrived(m_x1[0], rx1.at[0])
    p1[0, ring(x, 1), co] += rx1[0]
    send(m_xf[0, 0], p1.at[0, ring(x, 1), co], rxf.at[0, 0], at_x(1))
    arrived(m_x1[1], rx1.at[1])
    p1[1, ring(x, 3), co] += rx1[1]
    send(m_xf[1, 1], p1.at[1, ring(x, 3), co], rxf.at[1, 1], at_x(3))

    y_final(1)
    send(m_zf[0, 1], p2.at[y, ring(h, 1), 1], rzf.at[0, 1], at_h(1))
    y_final(2)
    send(m_zf[1, 0], p2.at[y, ring(h, 3), 0], rzf.at[1, 0], at_h(3))

    m_l = new()
    for k in range(2):
        for side in range(2):
            arrived(m_xf[side, k], rxf.at[side, k])
        p1[k, x, co] += rxf[0, k] + rxf[1, k]
    send(m_l, p1.at[1 - l, x, co], rl, at_l)

    arrived(m_z1[0], rz1.at[0])
    p2[y, ring(h, 1), 0] += rz1[0]
    send(m_zf[0, 0], p2.at[y, ring(h, 1), 0], rzf.at[0, 0], at_h(1))
    arrived(m_z1[1], rz1.at[1])
    p2[y, ring(h, 3), 1] += rz1[1]
    send(m_zf[1, 1], p2.at[y, ring(h, 3), 1], rzf.at[1, 1], at_h(3))

    def gather_row(buf):
        mz = new(4)
        my = [new(4) for _ in range(4)]

        def to_y(dh):
            mine = buf.at[y, ring(h, dh)]
            send(my[dh], mine, mine, at_y(1))
            send(my[dh] + 1, mine, mine, at_y(3))

        def y_step(dh):
            hs = ring(h, dh)
            got = buf.at[ring(y, 3), hs]
            arrived(my[dh], got)
            send(my[dh] + 2, got.at[0], got.at[0], at_y(1))
            got = buf.at[ring(y, 1), hs]
            arrived(my[dh] + 1, got)
            send(my[dh] + 3, got.at[1], got.at[1], at_y(3))

        mine = buf.at[y, h]
        send(mz, mine, mine, at_h(1))
        send(mz + 1, mine, mine, at_h(3))
        to_y(0)
        yield
        got = buf.at[y, ring(h, 3)]
        arrived(mz, got)
        send(mz + 2, got.at[0], got.at[0], at_h(1))
        to_y(3)
        got = buf.at[y, ring(h, 1)]
        arrived(mz + 1, got)
        send(mz + 3, got.at[1], got.at[1], at_h(3))
        to_y(1)
        yield
        y_step(0)
        yield
        got = buf.at[y, ring(h, 2)]
        arrived(mz + 2, got.at[0])
        arrived(mz + 3, got.at[1])
        to_y(2)
        yield
        y_step(3)
        y_step(1)
        yield
        y_step(2)
        yield
        for dh in (0, 3, 1, 2):
            got = buf.at[ring(y, 2), ring(h, dh)]
            arrived(my[dh] + 2, got.at[0])
            arrived(my[dh] + 3, got.at[1])
        yield

    def gather_col(buf):
        ml = new()
        mx = [new(4), new(4)]
        mc = new(8)

        def to_x(lk, k):
            mine = buf.at[lk, x, co]
            send(mx[k], mine, mine, at_x(1))
            send(mx[k] + 1, mine, mine, at_x(3))

        def to_co(lk, k, dx):
            mine = buf.at[lk, ring(x, dx), co]
            send(mc + k * 4 + dx, mine, mine, at_co)

        def x_step(lk, k):
            got = buf.at[lk, ring(x, 3), co]
            arrived(mx[k], got)
            send(mx[k] + 2, got.at[0], got.at[0], at_x(1))
            to_co(lk, k, 3)
            got = buf.at[lk, ring(x, 1), co]
            arrived(mx[k] + 1, got)
            send(mx[k] + 3, got.at[1], got.at[1], at_x(3))
            to_co(lk, k, 1)

        mine = buf.at[l, x, co]
        send(ml, mine, mine, at_l)
        to_x(l, 0)
        to_co(l, 0, 0)
        yield
        arrived(ml, buf.at[1 - l, x, co])
        to_x(1 - l, 1)
        to_co(1 - l, 1, 0)
        yield
        x_step(l, 0)
        yield
        x_step(1 - l, 1)
        yield
        for k, lk in enumerate((l, 1 - l)):
            got = buf.at[lk, ring(x, 2), co]
            arrived(mx[k] + 2, got.at[0])
            arrived(mx[k] + 3, got.at[1])
            to_co(lk, k, 2)
        yield
        for k, lk in enumerate((l, 1 - l)):
            for dx in range(4):
                arrived(mc + k * 4 + dx, buf.at[lk, ring(x, dx), 1 - co])
        yield

    arrived(m_l, rl)
    piece = p1[l, x, co] + rl[...]
    p1r[l, x, co] = piece.reshape(2, RANK, 128)
    m_t1 = new()

    @pl.when(off_diagonal)
    def _():
        copy(m_t1, p1r.at[l, x, co], p1t.at[c // 4, c % 4], at_t).start()

    @pl.when(jnp.logical_not(off_diagonal))
    def _():
        p1t[y, h] = p1r[l, x, co]

    ag_p1r = gather_col(p1r)
    next(ag_p1r)
    wide = jnp.concatenate([piece[:RANK], piece[RANK:]], 1)
    cy[y] = lax.dot(wide, wcore[...], precision=lax.Precision.HIGHEST, preferred_element_type=F32)
    m_cy = new(3)
    for d in (1, 2, 3):
        send(m_cy + d - 1, cy.at[y], cy.at[y], at_y(d))

    y_final(3)
    for s in (1, 0):
        for side in range(2):
            arrived(m_zf[side, s], rzf.at[side, s])
        p2c[y, h, s] = p2[y, h, s] + rzf[0, s] + rzf[1, s]
    m_t2 = new()

    @pl.when(off_diagonal)
    def _():
        copy(m_t2, p2c.at[y, h], p2r.at[r // 8, (r // 2) % 4, r % 2], at_t).start()

    @pl.when(jnp.logical_not(off_diagonal))
    def _():
        p2r[l, x, co] = p2c[y, h]

    ag_p2c = gather_row(p2c)
    next(ag_p2c)

    @pl.when(off_diagonal)
    def _():
        copy(m_t1, p1t.at[y, h], p1t.at[y, h], at_t).wait_recv()

    ag_p1t = gather_row(p1t)
    next(ag_p1t)
    next(ag_p1r)

    for d in (1, 2, 3):
        arrived(m_cy + d - 1, cy.at[ring(y, 4 - d)])
    cz[h] = cy[0] + cy[1] + cy[2] + cy[3]
    m_cz = new(3)
    for d in (1, 2, 3):
        send(m_cz + d - 1, cz.at[h], cz.at[h], at_h(d))

    next(ag_p1r)
    next(ag_p2c)

    @pl.when(off_diagonal)
    def _():
        copy(m_t2, p2r.at[l, x, co], p2r.at[l, x, co], at_t).wait_recv()

    ag_p2r = gather_col(p2r)
    next(ag_p2r)
    next(ag_p1t)
    next(ag_p1r)
    next(ag_p2c)
    next(ag_p2r)
    next(ag_p2c)
    next(ag_p1t)

    for d in (1, 2, 3):
        arrived(m_cz + d - 1, cz.at[ring(h, 4 - d)])
    cc[l, x, co] = cz[0] + cz[1] + cz[2] + cz[3]
    m_cx = new(3)
    for d in (1, 2, 3):
        send(m_cx + d - 1, cc.at[l, x, co], cc.at[l, x, co], at_x(d))

    next(ag_p2r)
    next(ag_p1t)
    next(ag_p2c)
    next(ag_p1r)
    next(ag_p2r)
    next(ag_p1t)
    for d in (1, 2, 3):
        arrived(m_cx + d - 1, cc.at[l, ring(x, 4 - d), co])
    m_cl = new()
    send(m_cl, cc.at[l, :, co], cc.at[l, :, co], at_l)
    next(ag_p2c)
    next(ag_p1t)
    next(ag_p1r)
    next(ag_p2r)
    arrived(m_cl, cc.at[1 - l, :, co])
    m_cc = new()
    send(m_cc, cc.at[:, :, co], cc.at[:, :, co], at_co)
    next(ag_p2r)
    next(ag_p1t)
    scale = 1.0 / (RANK * RANK)

    def gram(a, b):
        ah, al = split(a.T)
        bh, bl = split(b)
        left = jnp.concatenate([ah, al], 0)
        out = dot(left, bh, ((1,), (0,)))
        return out[:128] + out[128:] + dot(ah, bl, ((1,), (0,)))

    g = gram(p1r[...].reshape(1024, 128), p1t[...].reshape(1024, 128)) * scale
    g1_out[0] = g[:64, :64]
    g1_out[1] = g[64:, 64:]
    arrived(m_cc, cc.at[:, :, 1 - co])
    core_out[...] = cc[...].reshape(16, RANK, 128)
    next(ag_p2c)
    for s in range(2):
        a = p2c[:, :, s].reshape(1024, 128)
        b = p2r[:, :, :, s].reshape(1024, 128)
        g2_out[s] = gram(a, b) * scale

    for idx, src in sent:
        copy(idx, src, src, at_co).wait_send()

    @pl.when(off_diagonal)
    def _():
        copy(m_t1, p1r.at[l, x, co], p1r.at[l, x, co], at_t).wait_send()
        copy(m_t2, p2c.at[y, h], p2c.at[y, h], at_t).wait_send()

    assert counter[0] <= MESSAGES, counter[0]


MESSAGES = 160


def body(fields, factor_one, factor_two, factor_three):
    vmem = pl.BlockSpec(memory_space=pltpu.VMEM)

    def buf(*shape):
        return pltpu.VMEM((*shape, 128), F32)

    core, g1, g2 = pl.pallas_call(
        kernel,
        out_shape=(
            jax.ShapeDtypeStruct((16, RANK, 128), F32),
            jax.ShapeDtypeStruct((2, 64, 64), F32),
            jax.ShapeDtypeStruct((2, 128, 128), F32),
        ),
        in_specs=[pl.BlockSpec(memory_space=pl.ANY), vmem, vmem, vmem],
        out_specs=(vmem, vmem, vmem),
        scratch_shapes=[
            buf(CHUNKS, 16, 128), buf(4096), buf(4, 4, 2, 64), buf(2, 4, 2, 64), buf(256),
            buf(2, 4, 64), buf(2, 4, 2, 64), buf(2, 64), buf(2, 2, 64), buf(2, 4, 64), buf(2, 64), buf(2, 2, 64), buf(64),
            buf(4, 4, 2, 64), buf(4, 4, 2, 32), buf(2, 4, 2, 2, 64), buf(2, 4, 2, 2, 32),
            buf(4, 32), buf(4, 32), buf(2, 4, 2, 32),
            pltpu.SemaphoreType.DMA((CHUNKS,)),
            pltpu.SemaphoreType.DMA((MESSAGES,)),
            pltpu.SemaphoreType.DMA((MESSAGES,)),
        ],
        compiler_params=pltpu.CompilerParams(
            collective_id=0, has_side_effects=True, vmem_limit_bytes=48 << 20
        ),
        name="tucker",
    )(fields, factor_one, factor_two, factor_three)
    core = core.reshape(16, RANK, 2, 2, RANK).transpose(3, 4, 1, 2, 0).reshape(2, RANK, RANK, RANK)
    return core, g1, g2


def solution(mesh):
    placed = (P(None, "row", "col", None), P("row", None), P("col", None), P())
    return jax.shard_map(
        body,
        mesh=mesh,
        in_specs=placed,
        out_specs=(P(), P(None, "row", "col"), P(None, "col", "row")),
        check_vma=False,
    )
```

```python
import functools

import jax
import jax.numpy as jnp
from jax import lax
from jax.experimental import pallas as pl
from jax.experimental.pallas import tpu as pltpu
from jax.sharding import PartitionSpec as P

F32 = jnp.float32
BF16 = jnp.bfloat16
MESH = pl.DeviceIdType.MESH
RANK = 32
CHUNKS = 4


def split(x):
    high = x.astype(BF16)
    return high, (x - high.astype(F32)).astype(BF16)


def dot(a, b, dims):
    return lax.dot_general(a, b, ((dims[0], dims[1]), ((), ())), preferred_element_type=F32)


def stack_factor(f):
    high, low = split(f)
    return jnp.concatenate([jnp.concatenate([high, high], 1), jnp.concatenate([low, low], 1)], 0)


def kernel(
    fields, factors, core_out, g1_out, g2_out,
    xbuf, p3, p2, p1, wcore,
    ry1, ryf, rz1, rzf, rc1, rc2,
    p2c, p1t, p2r, p1r, cy, cz, cc,
    xsem, ss, rs,
):
    r, c = lax.axis_index("row"), lax.axis_index("col")
    y, h = r // 4, r % 4
    l, x, co = c // 8, (c // 2) % 4, c % 2

    def ring(v, d):
        return (v + d) % 4

    def at_y(d):
        return (ring(y, d) * 4 + h, c)

    def at_h(d):
        return (y * 4 + ring(h, d), c)

    def at_x(d):
        return (r, l * 8 + ring(x, d) * 2 + co)

    at_l = (r, (1 - l) * 8 + x * 2 + co)
    at_co = (r, l * 8 + x * 2 + (1 - co))
    x_r = (r // 2) % 4
    at_t2 = (c, (h // 2) * 8 + ring(y, x) * 2 + h % 2)
    at_t1 = ((ring(x, 4 - x_r)) * 4 + l * 2 + co, r)
    away = jnp.logical_or(at_t2[0] != r, at_t2[1] != c)

    def load(i):
        return pltpu.make_async_copy(fields.at[i // 2, pl.ds(i % 2 * 32, 32)], xbuf.at[i], xsem.at[i])

    for i in range(CHUNKS):
        load(i).start()
    barrier = pltpu.get_barrier_semaphore()
    def at_lx(d):
        return (r, (1 - l) * 8 + ring(x, d) * 2 + co)

    partners = [at(d) for at in (at_y, at_h, at_x, at_lx) for d in (1, 2, 3)] + [at_l, at_co]
    for to in partners:
        pl.semaphore_signal(barrier, inc=1, device_id=to, device_id_type=MESH)

    @pl.when(away)
    def _():
        pl.semaphore_signal(barrier, inc=1, device_id=at_t1, device_id_type=MESH)
        pl.semaphore_signal(barrier, inc=1, device_id=at_t2, device_id_type=MESH)

    sent = []

    def copy(idx, src, dst, to):
        return pltpu.make_async_remote_copy(
            src_ref=src, dst_ref=dst, send_sem=ss.at[idx], recv_sem=rs.at[idx], device_id=to, device_id_type=MESH
        )

    counter = [0]

    def new(n=1):
        counter[0] += n
        return counter[0] - n

    def send(idx, src, dst, to):
        copy(idx, src, dst, to).start()
        sent.append((idx, src))

    def arrived(idx, dst):
        copy(idx, dst, dst, at_co).wait_recv()

    f3, f1, f2 = factors[:, :128], factors[:, 256:320], factors[:, 128:256]
    l3, l1, l2 = stack_factor(f3), stack_factor(f1), stack_factor(f2)
    wcore[...] = jnp.zeros_like(wcore)
    for b in range(4):
        wcore[pl.ds(b * 32, 32), pl.ds(b * 64, 64)] = f1

    def project(i, _):
        load(i).wait()
        for n in range(16):
            high, low = split(xbuf[i, pl.ds(n * 2, 2)].reshape(256, 128))
            out = dot(l3, jnp.concatenate([high, low], 1), ((1,), (1,)))
            out = out[:RANK] + out[RANK:]
            at = pl.multiple_of(i * 32 * RANK, RANK) + n * 2 * RANK
            p3[pl.ds(at, RANK), :] = out[:, :128]
            p3[pl.ds(at + RANK, RANK), :] = out[:, 128:]
        return 0

    lax.fori_loop(0, CHUNKS, project, 0)

    def slot_products(ys, hs):
        k = ys * 4 + hs
        halves = []
        for t2 in range(2):
            tile = p3[pl.ds(k + 16 * t2, 128, stride=RANK), :]
            halves.append(split(tile))
        right = [jnp.concatenate([jnp.concatenate([hi[s * 64:s * 64 + 64], lo[s * 64:s * 64 + 64]], 0) for s in range(2)], 1) for hi, lo in halves]
        out = dot(l1, jnp.concatenate(right, 1), ((1,), (0,)))
        out = out[:RANK] + out[RANK:]
        for t2 in range(2):
            for s in range(2):
                at = t2 * 256 + s * 128
                p2[ys, hs, s, pl.ds(t2 * RANK, RANK), :] = out[:, at:at + 128]
        right = jnp.concatenate([jnp.concatenate([hi, lo], 1) for hi, lo in halves], 0)
        out = dot(l2, right, ((1,), (1,)))
        out = out[:RANK] + out[RANK:]
        lk, xk, ck = k // 8, (k // 2) % 4, k % 2
        for t2 in range(2):
            p1[lk, xk, ck, pl.ds(t2 * RANK, RANK), :] = out[:, t2 * 128:t2 * 128 + 128]

    pl.semaphore_wait(barrier, len(partners) + jnp.where(away, 2, 0))

    order = (2, 1, 3, 0)
    m_y1 = [new(4), new(4)]
    m_yf = {(side, s): new(4) for side in range(2) for s in range(2)}

    for dy in order:
        for n, dh in enumerate(order):
            ys, hs = ring(y, dy), ring(h, dh)
            slot_products(ys, hs)
            if dy == 2:
                send(m_y1[0] + n, p2.at[ys, hs, 0], ry1.at[0, hs], at_y(1))
                send(m_y1[1] + n, p2.at[ys, hs, 1], ry1.at[1, hs], at_y(3))

    def y_late(n):
        hs = ring(h, order[n])
        up, down = ring(y, 1), ring(y, 3)
        send(m_yf[0, 1] + n, p2.at[up, hs, 1], ryf.at[0, hs, 1], at_y(1))
        send(m_yf[1, 0] + n, p2.at[down, hs, 0], ryf.at[1, hs, 0], at_y(3))
        arrived(m_y1[0] + n, ry1.at[0, hs])
        p2[up, hs, 0] += ry1[0, hs]
        send(m_yf[0, 0] + n, p2.at[up, hs, 0], ryf.at[0, hs, 0], at_y(1))
        arrived(m_y1[1] + n, ry1.at[1, hs])
        p2[down, hs, 1] += ry1[1, hs]
        send(m_yf[1, 1] + n, p2.at[down, hs, 1], ryf.at[1, hs, 1], at_y(3))

    def y_final(n):
        hs = ring(h, order[n])
        for s in (1, 0):
            for side in range(2):
                arrived(m_yf[side, s] + n, ryf.at[side, hs, s])
            p2[y, hs, s] += ryf[0, hs, s] + ryf[1, hs, s]

    def gather_row(buf):
        mz = new(4)
        my = [new(4) for _ in range(4)]

        def to_y(dh):
            mine = buf.at[y, ring(h, dh)]
            send(my[dh], mine, mine, at_y(1))
            send(my[dh] + 1, mine, mine, at_y(3))

        def y_step(dh):
            hs = ring(h, dh)
            got = buf.at[ring(y, 3), hs]
            arrived(my[dh], got)
            send(my[dh] + 2, got.at[0], got.at[0], at_y(1))
            got = buf.at[ring(y, 1), hs]
            arrived(my[dh] + 1, got)
            send(my[dh] + 3, got.at[1], got.at[1], at_y(3))

        mine = buf.at[y, h]
        send(mz, mine, mine, at_h(1))
        send(mz + 1, mine, mine, at_h(3))
        to_y(0)
        yield
        y_step(0)
        yield
        got = buf.at[y, ring(h, 3)]
        arrived(mz, got)
        send(mz + 2, got.at[0], got.at[0], at_h(1))
        to_y(3)
        got = buf.at[y, ring(h, 1)]
        arrived(mz + 1, got)
        send(mz + 3, got.at[1], got.at[1], at_h(3))
        to_y(1)
        yield
        got = buf.at[y, ring(h, 2)]
        arrived(mz + 2, got.at[0])
        arrived(mz + 3, got.at[1])
        to_y(2)
        yield
        y_step(3)
        y_step(1)
        yield
        y_step(2)
        yield
        for dh in (0, 3, 1, 2):
            got = buf.at[ring(y, 2), ring(h, dh)]
            arrived(my[dh] + 2, got.at[0])
            arrived(my[dh] + 3, got.at[1])
        yield

    def gather_col(buf):
        ml = new()
        mx = [new(4), new(4)]
        mc = new(8)

        def to_x(lk, k):
            mine = buf.at[lk, x, co]
            send(mx[k], mine, mine, at_x(1))
            send(mx[k] + 1, mine, mine, at_x(3))

        def to_co(lk, k, dx):
            mine = buf.at[lk, ring(x, dx), co]
            send(mc + k * 4 + dx, mine, mine, at_co)

        def x_step(lk, k):
            got = buf.at[lk, ring(x, 3), co]
            arrived(mx[k], got)
            send(mx[k] + 2, got.at[0], got.at[0], at_x(1))
            to_co(lk, k, 3)
            got = buf.at[lk, ring(x, 1), co]
            arrived(mx[k] + 1, got)
            send(mx[k] + 3, got.at[1], got.at[1], at_x(3))
            to_co(lk, k, 1)

        mine = buf.at[l, x, co]
        send(ml, mine, mine, at_l)
        to_x(l, 0)
        to_co(l, 0, 0)
        yield
        arrived(ml, buf.at[1 - l, x, co])
        to_x(1 - l, 1)
        to_co(1 - l, 1, 0)
        yield
        x_step(l, 0)
        yield
        x_step(1 - l, 1)
        yield
        for k, lk in enumerate((l, 1 - l)):
            got = buf.at[lk, ring(x, 2), co]
            arrived(mx[k] + 2, got.at[0])
            arrived(mx[k] + 3, got.at[1])
            to_co(lk, k, 2)
        yield
        for k, lk in enumerate((l, 1 - l)):
            for dx in range(4):
                arrived(mc + k * 4 + dx, buf.at[lk, ring(x, dx), 1 - co])
        yield

    m_core = new()
    send(m_core, p1.at[:, :, 1 - co], rc1, at_co)
    y_late(0)
    arrived(m_core, rc1)
    for lk in range(2):
        for xk in range(4):
            p1[lk, xk, co] += rc1[lk, xk]
    m_x = new(8)
    for d in (2, 1, 3):
        send(m_x + d, p1.at[l, ring(x, d), co], rc2.at[d], at_x(d))
        send(m_x + 4 + d, p1.at[1 - l, ring(x, d), co], rc2.at[4 + d], at_lx(d))
    send(m_x + 4, p1.at[1 - l, x, co], rc2.at[4], at_l)

    for n in range(1, 4):
        y_late(n)

    m_z1 = [new(), new()]
    m_zf = {(side, s): new() for side in range(2) for s in range(2)}
    y_final(0)
    send(m_z1[0], p2.at[y, ring(h, 2), 0], rz1.at[0], at_h(1))
    send(m_z1[1], p2.at[y, ring(h, 2), 1], rz1.at[1], at_h(3))
    y_final(1)
    send(m_zf[0, 1], p2.at[y, ring(h, 1), 1], rzf.at[0, 1], at_h(1))

    piece = p1[l, x, co]
    for k in range(1, 8):
        arrived(m_x + k, rc2.at[k])
        piece = piece + rc2[k]
    p1r[l, x, co] = piece.reshape(2, RANK, 128)
    m_t1, m_t2 = new(), new()

    @pl.when(away)
    def _():
        copy(m_t1, p1r.at[l, x, co], p1t.at[ring(x, 4 - x_r), l * 2 + co], at_t1).start()

    @pl.when(jnp.logical_not(away))
    def _():
        p1t[y, h] = p1r[l, x, co]

    ag_p1r = gather_col(p1r)
    next(ag_p1r)
    wide = jnp.concatenate([piece[:RANK], piece[RANK:]], 1)
    cy[y] = lax.dot_general(wide, wcore[...], (((1,), (1,)), ((), ())), precision=lax.Precision.HIGHEST, preferred_element_type=F32)
    m_cy, m_cz, m_cx = new(3), new(3), new(3)
    for d in (2, 1, 3):
        send(m_cy + d - 1, cy.at[y], cy.at[y], at_y(d))

    y_final(2)
    send(m_zf[1, 0], p2.at[y, ring(h, 3), 0], rzf.at[1, 0], at_h(3))
    arrived(m_z1[0], rz1.at[0])
    p2[y, ring(h, 1), 0] += rz1[0]
    send(m_zf[0, 0], p2.at[y, ring(h, 1), 0], rzf.at[0, 0], at_h(1))
    arrived(m_z1[1], rz1.at[1])
    p2[y, ring(h, 3), 1] += rz1[1]
    send(m_zf[1, 1], p2.at[y, ring(h, 3), 1], rzf.at[1, 1], at_h(3))
    y_final(3)
    next(ag_p1r)

    for d in (1, 2, 3):
        arrived(m_cy + d - 1, cy.at[ring(y, 4 - d)])
    cz[h] = cy[0] + cy[1] + cy[2] + cy[3]
    for d in (2, 1, 3):
        send(m_cz + d - 1, cz.at[h], cz.at[h], at_h(d))
    next(ag_p1r)

    for s in (1, 0):
        for side in range(2):
            arrived(m_zf[side, s], rzf.at[side, s])
        p2c[y, h, s] = p2[y, h, s] + rzf[0, s] + rzf[1, s]

    @pl.when(away)
    def _():
        copy(m_t2, p2c.at[y, h], p2r.at[h // 2, ring(y, x), h % 2], at_t2).start()

    @pl.when(jnp.logical_not(away))
    def _():
        p2r[l, x, co] = p2c[y, h]

    ag_p2c = gather_row(p2c)
    next(ag_p2c)

    @pl.when(away)
    def _():
        copy(m_t1, p1t.at[y, h], p1t.at[y, h], at_t2).wait_recv()

    ag_p1t = gather_row(p1t)
    next(ag_p1t)
    next(ag_p1r)
    for d in (1, 2, 3):
        arrived(m_cz + d - 1, cz.at[ring(h, 4 - d)])
    cc[l, x, co] = cz[0] + cz[1] + cz[2] + cz[3]
    for d in (2, 1, 3):
        send(m_cx + d - 1, cc.at[l, x, co], cc.at[l, x, co], at_x(d))
    next(ag_p1r)
    next(ag_p2c)
    next(ag_p1t)
    next(ag_p1t)

    @pl.when(away)
    def _():
        copy(m_t2, p2r.at[l, x, co], p2r.at[l, x, co], at_t2).wait_recv()

    ag_p2r = gather_col(p2r)
    next(ag_p2r)
    next(ag_p2c)
    for d in (1, 2, 3):
        arrived(m_cx + d - 1, cc.at[l, ring(x, 4 - d), co])
    m_cl, m_cc = new(), new()
    send(m_cl, cc.at[l, :, co], cc.at[l, :, co], at_l)
    next(ag_p1t)
    next(ag_p2r)
    next(ag_p2r)
    next(ag_p2c)
    next(ag_p2c)
    next(ag_p1t)
    arrived(m_cl, cc.at[1 - l, :, co])
    send(m_cc, cc.at[:, :, co], cc.at[:, :, co], at_co)
    next(ag_p2r)
    next(ag_p2c)
    next(ag_p1t)
    next(ag_p2r)
    scale = 1.0 / (RANK * RANK)

    def gram(a, b):
        ah, al = split(a.T)
        bh, bl = split(b)
        left = jnp.concatenate([ah, al], 0)
        out = dot(left, bh, ((1,), (0,)))
        return out[:128] + out[128:] + dot(ah, bl, ((1,), (0,)))

    next(ag_p1r)
    next(ag_p1t)
    g = sum(gram(p1r[:, ring(x, d)].reshape(256, 128), p1t[d].reshape(256, 128)) for d in range(4)) * scale
    g1_out[0] = g[:64, :64]
    g1_out[1] = g[64:, 64:]

    arrived(m_cc, cc.at[:, :, 1 - co])
    flat = cc.reshape(16 * RANK, 128)
    for q4 in range(8):
        rows = []
        for j in range(4):
            mine = flat[pl.ds(q4 * 4 + j, 16, stride=RANK), :]
            rows.extend((mine[:, :64], mine[:, 64:]))
        turned = jnp.concatenate(rows, 0).T
        for j in range(4):
            core_out[pl.ds(q4 * 4 + j, 64, stride=RANK), :] = turned[:, j * RANK:(j + 1) * RANK]
    next(ag_p2r)

    def partial(dy):
        ys = ring(y, dy)
        return [
            gram(
                p2c[ys, :, s].reshape(256, 128),
                p2r[:, ring(ys, x_r), :, s].reshape(256, 128),
            )
            for s in range(2)
        ]

    total = [partial(dy) for dy in (0, 1, 3)]
    next(ag_p2c)
    total.append(partial(2))
    for s in range(2):
        g2_out[s] = sum(t[s] for t in total) * scale

    for idx, src in sent:
        copy(idx, src, src, at_co).wait_send()

    @pl.when(away)
    def _():
        copy(m_t1, p1r.at[l, x, co], p1r.at[l, x, co], at_t2).wait_send()
        copy(m_t2, p2c.at[y, h], p2c.at[y, h], at_t2).wait_send()

    assert counter[0] <= MESSAGES, counter[0]


MESSAGES = 160


def body(fields, factor_one, factor_two, factor_three):
    vmem = pl.BlockSpec(memory_space=pltpu.VMEM)

    def buf(*shape):
        return pltpu.VMEM((*shape, 128), F32)

    core, g1, g2 = pl.pallas_call(
        kernel,
        out_shape=(
            jax.ShapeDtypeStruct((2 * RANK * RANK, RANK), F32),
            jax.ShapeDtypeStruct((2, 64, 64), F32),
            jax.ShapeDtypeStruct((2, 128, 128), F32),
        ),
        in_specs=[pl.BlockSpec(memory_space=pl.ANY), vmem],
        out_specs=(vmem, vmem, vmem),
        scratch_shapes=[
            buf(CHUNKS, 32, 128), buf(4096), buf(4, 4, 2, 64), buf(2, 4, 2, 64), pltpu.VMEM((128, 256), F32),
            buf(2, 4, 64), buf(2, 4, 2, 64), buf(2, 64), buf(2, 2, 64), buf(2, 4, 64), buf(8, 64),
            buf(4, 4, 2, 64), buf(4, 4, 2, 32), buf(2, 4, 2, 2, 64), buf(2, 4, 2, 2, 32),
            buf(4, 32), buf(4, 32), buf(2, 4, 2, 32),
            pltpu.SemaphoreType.DMA((CHUNKS,)),
            pltpu.SemaphoreType.DMA((MESSAGES,)),
            pltpu.SemaphoreType.DMA((MESSAGES,)),
        ],
        compiler_params=pltpu.CompilerParams(
            collective_id=0, has_side_effects=True, vmem_limit_bytes=48 << 20
        ),
        name="tucker",
    )(fields, jnp.concatenate([factor_three.T, factor_two.T, factor_one.T], 1))
    return core.reshape(2, RANK, RANK, RANK), g1, g2


def solution(mesh):
    placed = (P(None, "row", "col", None), P("row", None), P("col", None), P())
    return jax.shard_map(
        body,
        mesh=mesh,
        in_specs=placed,
        out_specs=(P(), P(None, "row", "col"), P(None, "col", "row")),
        check_vma=False,
    )
```

```python
import functools

import jax
import jax.numpy as jnp
from jax import lax
from jax.experimental import pallas as pl
from jax.experimental.pallas import tpu as pltpu
from jax.sharding import PartitionSpec as P

F32 = jnp.float32
BF16 = jnp.bfloat16
MESH = pl.DeviceIdType.MESH
RANK = 32
CHUNKS = 4


def split(x):
    high = x.astype(BF16)
    return high, (x - high.astype(F32)).astype(BF16)


def dot(a, b, dims):
    return lax.dot_general(a, b, ((dims[0], dims[1]), ((), ())), preferred_element_type=F32)


def stack_factor(f):
    high, low = split(f)
    return jnp.concatenate([jnp.concatenate([high, high], 1), jnp.concatenate([low, low], 1)], 0)


def kernel(
    fields, factors, core_out, g1_out, g2_out,
    xbuf, p3, p2, p1, wcore,
    ry1, ryf, rz1, rzf, rc1, rc2,
    p2c, p1t, p2r, p1r, cy, cz, cc,
    xsem, ss, rs,
):
    r, c = lax.axis_index("row"), lax.axis_index("col")
    y, h = r // 4, r % 4
    l, x, co = c // 8, (c // 2) % 4, c % 2

    def ring(v, d):
        return (v + d) % 4

    def at_y(d):
        return (ring(y, d) * 4 + h, c)

    def at_h(d):
        return (y * 4 + ring(h, d), c)

    def at_x(d):
        return (r, l * 8 + ring(x, d) * 2 + co)

    at_l = (r, (1 - l) * 8 + x * 2 + co)
    at_co = (r, l * 8 + x * 2 + (1 - co))
    x_r = (r // 2) % 4
    at_t2 = (c, (h // 2) * 8 + ring(y, x) * 2 + h % 2)
    at_t1 = ((ring(x, 4 - x_r)) * 4 + l * 2 + co, r)
    away = jnp.logical_or(at_t2[0] != r, at_t2[1] != c)

    def load(i):
        return pltpu.make_async_copy(fields.at[i // 2, pl.ds(i % 2 * 32, 32)], xbuf.at[i], xsem.at[i])

    for i in range(CHUNKS):
        load(i).start()
    barrier = pltpu.get_barrier_semaphore()
    def at_lx(d):
        return (r, (1 - l) * 8 + ring(x, d) * 2 + co)

    partners = [at(d) for at in (at_y, at_h, at_x, at_lx) for d in (1, 2, 3)] + [at_l, at_co]
    for to in partners:
        pl.semaphore_signal(barrier, inc=1, device_id=to, device_id_type=MESH)

    @pl.when(away)
    def _():
        pl.semaphore_signal(barrier, inc=1, device_id=at_t1, device_id_type=MESH)
        pl.semaphore_signal(barrier, inc=1, device_id=at_t2, device_id_type=MESH)

    sent = []

    def copy(idx, src, dst, to):
        return pltpu.make_async_remote_copy(
            src_ref=src, dst_ref=dst, send_sem=ss.at[idx], recv_sem=rs.at[idx], device_id=to, device_id_type=MESH
        )

    counter = [0]

    def new(n=1):
        counter[0] += n
        return counter[0] - n

    def send(idx, src, dst, to):
        copy(idx, src, dst, to).start()
        sent.append((idx, src))

    def arrived(idx, dst):
        copy(idx, dst, dst, at_co).wait_recv()

    f3, f1, f2 = factors[:, :128], factors[:, 256:320], factors[:, 128:256]
    l3, l1, l2 = stack_factor(f3), stack_factor(f1), stack_factor(f2)
    wcore[...] = jnp.zeros_like(wcore)
    for b in range(4):
        wcore[pl.ds(b * 32, 32), pl.ds(b * 64, 64)] = f1

    def project(i, _):
        load(i).wait()
        for n in range(16):
            high, low = split(xbuf[i, pl.ds(n * 2, 2)].reshape(256, 128))
            out = dot(l3, jnp.concatenate([high, low], 1), ((1,), (1,)))
            out = out[:RANK] + out[RANK:]
            at = pl.multiple_of(i * 32 * RANK, RANK) + n * 2 * RANK
            p3[pl.ds(at, RANK), :] = out[:, :128]
            p3[pl.ds(at + RANK, RANK), :] = out[:, 128:]
        return 0

    lax.fori_loop(0, CHUNKS, project, 0)

    def mode_two(ys, hs):
        k = ys * 4 + hs
        right = []
        for half in range(2):
            hi, lo = split(p3[pl.ds(k + 16 * half, 128, stride=RANK), :])
            right.extend(jnp.concatenate([hi[s * 64:s * 64 + 64], lo[s * 64:s * 64 + 64]], 0) for s in range(2))
        out = dot(l1, jnp.concatenate(right, 1), ((1,), (0,)))
        out = out[:RANK] + out[RANK:]
        for half in range(2):
            for s in range(2):
                at = half * 256 + s * 128
                p2[ys, hs, s, pl.ds(half * RANK, RANK), :] = out[:, at:at + 128]

    def mode_one(k):
        parts = [jnp.concatenate(split(p3[pl.ds(half * 16 + k, 128, stride=RANK), :]), 1) for half in range(2)]
        out = dot(l2, jnp.concatenate(parts, 0), ((1,), (1,)))
        out = out[:RANK] + out[RANK:]
        for half in range(2):
            p1[k // 8, (k // 2) % 4, k % 2, pl.ds(half * RANK, RANK), :] = out[:, half * 128:half * 128 + 128]

    pl.semaphore_wait(barrier, len(partners) + jnp.where(away, 2, 0))

    order = (2, 1, 3, 0)
    m_y1 = [new(4), new(4)]
    m_yf = {(side, s): new(4) for side in range(2) for s in range(2)}

    m_core, m_x = new(), new(8)
    for k in range(16):
        mode_one(k)
    send(m_core, p1.at[:, :, 1 - co], rc1, at_co)
    for dy in order:
        if dy == 3:
            arrived(m_core, rc1)
            for lk in range(2):
                for xk in range(4):
                    p1[lk, xk, co] += rc1[lk, xk]
            for d in (2, 1, 3):
                send(m_x + d, p1.at[l, ring(x, d), co], rc2.at[d], at_x(d))
                send(m_x + 4 + d, p1.at[1 - l, ring(x, d), co], rc2.at[4 + d], at_lx(d))
            send(m_x + 4, p1.at[1 - l, x, co], rc2.at[4], at_l)
        for n, dh in enumerate(order):
            ys, hs = ring(y, dy), ring(h, dh)
            mode_two(ys, hs)
            if dy == 2:
                send(m_y1[0] + n, p2.at[ys, hs, 0], ry1.at[0, hs], at_y(1))
                send(m_y1[1] + n, p2.at[ys, hs, 1], ry1.at[1, hs], at_y(3))

    def y_late(n):
        hs = ring(h, order[n])
        up, down = ring(y, 1), ring(y, 3)
        send(m_yf[0, 1] + n, p2.at[up, hs, 1], ryf.at[0, hs, 1], at_y(1))
        send(m_yf[1, 0] + n, p2.at[down, hs, 0], ryf.at[1, hs, 0], at_y(3))
        arrived(m_y1[0] + n, ry1.at[0, hs])
        p2[up, hs, 0] += ry1[0, hs]
        send(m_yf[0, 0] + n, p2.at[up, hs, 0], ryf.at[0, hs, 0], at_y(1))
        arrived(m_y1[1] + n, ry1.at[1, hs])
        p2[down, hs, 1] += ry1[1, hs]
        send(m_yf[1, 1] + n, p2.at[down, hs, 1], ryf.at[1, hs, 1], at_y(3))

    def y_final(n):
        hs = ring(h, order[n])
        for s in (1, 0):
            for side in range(2):
                arrived(m_yf[side, s] + n, ryf.at[side, hs, s])
            p2[y, hs, s] += ryf[0, hs, s] + ryf[1, hs, s]

    def gather_row(buf):
        mz = new(6)
        my = [new(4) for _ in range(4)]

        def to_y(dh):
            mine = buf.at[y, ring(h, dh)]
            send(my[dh], mine, mine, at_y(1))
            send(my[dh] + 1, mine, mine, at_y(3))

        def y_step(dh):
            hs = ring(h, dh)
            got = buf.at[ring(y, 3), hs]
            arrived(my[dh], got)
            send(my[dh] + 2, got.at[0], got.at[0], at_y(1))
            got = buf.at[ring(y, 1), hs]
            arrived(my[dh] + 1, got)
            send(my[dh] + 3, got.at[1], got.at[1], at_y(3))

        mine = buf.at[y, h]
        for half in range(2):
            send(mz + 4 * half, mine.at[half], mine.at[half], at_h(1))
            send(mz + 1 + 4 * half, mine.at[1 - half], mine.at[1 - half], at_h(3))
        to_y(0)
        yield
        y_step(0)
        yield
        below, above = buf.at[y, ring(h, 3)], buf.at[y, ring(h, 1)]
        arrived(mz, below.at[0])
        send(mz + 2, below.at[0], below.at[0], at_h(1))
        arrived(mz + 1, above.at[1])
        send(mz + 3, above.at[1], above.at[1], at_h(3))
        arrived(mz + 4, below.at[1])
        to_y(3)
        arrived(mz + 5, above.at[0])
        to_y(1)
        yield
        got = buf.at[y, ring(h, 2)]
        arrived(mz + 2, got.at[0])
        arrived(mz + 3, got.at[1])
        to_y(2)
        yield
        y_step(3)
        y_step(1)
        yield
        y_step(2)
        yield
        for dh in (0, 3, 1, 2):
            got = buf.at[ring(y, 2), ring(h, dh)]
            arrived(my[dh] + 2, got.at[0])
            arrived(my[dh] + 3, got.at[1])
        yield

    def gather_col(buf):
        ml = new()
        mx = [new(4), new(4)]
        mc = new(8)

        def to_x(lk, k):
            mine = buf.at[lk, x, co]
            send(mx[k], mine, mine, at_x(1))
            send(mx[k] + 1, mine, mine, at_x(3))
            if k:
                send(mx[k] + 2, mine, mine, at_x(2))

        def to_co(lk, k, dx):
            mine = buf.at[lk, ring(x, dx), co]
            send(mc + k * 4 + dx, mine, mine, at_co)

        def x_step(lk, k):
            got = buf.at[lk, ring(x, 3), co]
            arrived(mx[k], got)
            if not k:
                send(mx[k] + 2, got.at[0], got.at[0], at_x(1))
            to_co(lk, k, 3)
            got = buf.at[lk, ring(x, 1), co]
            arrived(mx[k] + 1, got)
            if not k:
                send(mx[k] + 3, got.at[1], got.at[1], at_x(3))
            to_co(lk, k, 1)

        mine = buf.at[l, x, co]
        send(ml, mine, mine, at_l)
        to_x(l, 0)
        to_co(l, 0, 0)
        yield
        arrived(ml, buf.at[1 - l, x, co])
        to_x(1 - l, 1)
        to_co(1 - l, 1, 0)
        yield
        x_step(l, 0)
        yield
        x_step(1 - l, 1)
        yield
        for k, lk in enumerate((l, 1 - l)):
            got = buf.at[lk, ring(x, 2), co]
            if k:
                arrived(mx[k] + 2, got)
            else:
                arrived(mx[k] + 2, got.at[0])
                arrived(mx[k] + 3, got.at[1])
            to_co(lk, k, 2)
        yield
        for k, lk in enumerate((l, 1 - l)):
            for dx in range(4):
                arrived(mc + k * 4 + dx, buf.at[lk, ring(x, dx), 1 - co])
        yield

    for n in range(4):
        y_late(n)

    m_z1 = [new(), new()]
    m_zf = {(side, s): new() for side in range(2) for s in range(2)}
    y_final(0)
    send(m_z1[0], p2.at[y, ring(h, 2), 0], rz1.at[0], at_h(1))
    send(m_z1[1], p2.at[y, ring(h, 2), 1], rz1.at[1], at_h(3))
    piece = p1[l, x, co]
    for k in range(1, 8):
        arrived(m_x + k, rc2.at[k])
        piece = piece + rc2[k]
    p1r[l, x, co] = piece.reshape(2, RANK, 128)
    m_t1, m_t2 = new(), new()

    @pl.when(away)
    def _():
        copy(m_t1, p1r.at[l, x, co], p1t.at[ring(x, 4 - x_r), l * 2 + co], at_t1).start()

    @pl.when(jnp.logical_not(away))
    def _():
        p1t[y, h] = p1r[l, x, co]

    ag_p1r = gather_col(p1r)
    next(ag_p1r)
    wide = jnp.concatenate([piece[:RANK], piece[RANK:]], 1)
    cy[y] = lax.dot_general(wide, wcore[...], (((1,), (1,)), ((), ())), precision=lax.Precision.HIGHEST, preferred_element_type=F32)
    m_cy, m_cz, m_cx = new(3), new(3), new(3)
    for d in (2, 1, 3):
        send(m_cy + d - 1, cy.at[y], cy.at[y], at_y(d))

    y_final(1)
    send(m_zf[0, 1], p2.at[y, ring(h, 1), 1], rzf.at[0, 1], at_h(1))

    y_final(2)
    send(m_zf[1, 0], p2.at[y, ring(h, 3), 0], rzf.at[1, 0], at_h(3))
    arrived(m_z1[0], rz1.at[0])
    p2[y, ring(h, 1), 0] += rz1[0]
    send(m_zf[0, 0], p2.at[y, ring(h, 1), 0], rzf.at[0, 0], at_h(1))
    arrived(m_z1[1], rz1.at[1])
    p2[y, ring(h, 3), 1] += rz1[1]
    send(m_zf[1, 1], p2.at[y, ring(h, 3), 1], rzf.at[1, 1], at_h(3))
    y_final(3)
    next(ag_p1r)

    for d in (1, 2, 3):
        arrived(m_cy + d - 1, cy.at[ring(y, 4 - d)])
    cz[h] = cy[0] + cy[1] + cy[2] + cy[3]
    for d in (2, 1, 3):
        send(m_cz + d - 1, cz.at[h], cz.at[h], at_h(d))
    next(ag_p1r)

    for s in (1, 0):
        for side in range(2):
            arrived(m_zf[side, s], rzf.at[side, s])
        p2c[y, h, s] = p2[y, h, s] + rzf[0, s] + rzf[1, s]

    @pl.when(away)
    def _():
        copy(m_t2, p2c.at[y, h], p2r.at[h // 2, ring(y, x), h % 2], at_t2).start()

    @pl.when(jnp.logical_not(away))
    def _():
        p2r[l, x, co] = p2c[y, h]

    ag_p2c = gather_row(p2c)
    next(ag_p2c)

    @pl.when(away)
    def _():
        copy(m_t1, p1t.at[y, h], p1t.at[y, h], at_t2).wait_recv()

    ag_p1t = gather_row(p1t)
    next(ag_p1t)
    next(ag_p1r)
    for d in (1, 2, 3):
        arrived(m_cz + d - 1, cz.at[ring(h, 4 - d)])
    cc[l, x, co] = cz[0] + cz[1] + cz[2] + cz[3]
    for d in (2, 1, 3):
        send(m_cx + d - 1, cc.at[l, x, co], cc.at[l, x, co], at_x(d))
    next(ag_p1r)
    next(ag_p2c)
    @pl.when(away)
    def _():
        copy(m_t2, p2r.at[l, x, co], p2r.at[l, x, co], at_t2).wait_recv()

    ag_p2r = gather_col(p2r)
    next(ag_p2r)
    next(ag_p1t)

    next(ag_p2c)
    next(ag_p1t)
    for d in (1, 2, 3):
        arrived(m_cx + d - 1, cc.at[l, ring(x, 4 - d), co])
    m_cl, m_cc = new(), new()
    send(m_cl, cc.at[l, :, co], cc.at[l, :, co], at_l)
    next(ag_p1t)
    next(ag_p2r)
    next(ag_p2r)
    next(ag_p2c)
    next(ag_p2c)
    next(ag_p1t)
    arrived(m_cl, cc.at[1 - l, :, co])
    send(m_cc, cc.at[:, :, co], cc.at[:, :, co], at_co)
    next(ag_p2r)
    next(ag_p2c)
    next(ag_p1t)
    next(ag_p2r)
    scale = 1.0 / (RANK * RANK)

    def gram(a, b):
        ah, al = split(a.T)
        bh, bl = split(b)
        left = jnp.concatenate([ah, al], 0)
        out = dot(left, bh, ((1,), (0,)))
        return out[:128] + out[128:] + dot(ah, bl, ((1,), (0,)))

    next(ag_p1r)
    next(ag_p1t)
    g = sum(gram(p1r[:, ring(x, d)].reshape(256, 128), p1t[d].reshape(256, 128)) for d in range(4)) * scale
    g1_out[0] = g[:64, :64]
    g1_out[1] = g[64:, 64:]

    arrived(m_cc, cc.at[:, :, 1 - co])
    flat = cc.reshape(16 * RANK, 128)
    for q4 in range(8):
        rows = []
        for j in range(4):
            mine = flat[pl.ds(q4 * 4 + j, 16, stride=RANK), :]
            rows.extend((mine[:, :64], mine[:, 64:]))
        turned = jnp.concatenate(rows, 0).T
        for j in range(4):
            core_out[pl.ds(q4 * 4 + j, 64, stride=RANK), :] = turned[:, j * RANK:(j + 1) * RANK]
    next(ag_p2r)

    def partial(dy):
        ys = ring(y, dy)
        return [
            gram(
                p2c[ys, :, s].reshape(256, 128),
                p2r[:, ring(ys, x_r), :, s].reshape(256, 128),
            )
            for s in range(2)
        ]

    early = len(sent) - 12
    for idx, src in sent[:early]:
        copy(idx, src, src, at_co).wait_send()
    total = [partial(dy) for dy in (0, 1, 3)]
    next(ag_p2c)
    total.append(partial(2))
    for s in range(2):
        g2_out[s] = sum(t[s] for t in total) * scale

    for idx, src in sent[early:]:
        copy(idx, src, src, at_co).wait_send()

    @pl.when(away)
    def _():
        copy(m_t1, p1r.at[l, x, co], p1r.at[l, x, co], at_t2).wait_send()
        copy(m_t2, p2c.at[y, h], p2c.at[y, h], at_t2).wait_send()

    assert counter[0] <= MESSAGES, counter[0]


MESSAGES = 160


def body(fields, factor_one, factor_two, factor_three):
    vmem = pl.BlockSpec(memory_space=pltpu.VMEM)

    def buf(*shape):
        return pltpu.VMEM((*shape, 128), F32)

    core, g1, g2 = pl.pallas_call(
        kernel,
        out_shape=(
            jax.ShapeDtypeStruct((2 * RANK * RANK, RANK), F32),
            jax.ShapeDtypeStruct((2, 64, 64), F32),
            jax.ShapeDtypeStruct((2, 128, 128), F32),
        ),
        in_specs=[pl.BlockSpec(memory_space=pl.ANY), vmem],
        out_specs=(vmem, vmem, vmem),
        scratch_shapes=[
            buf(CHUNKS, 32, 128), buf(4096), buf(4, 4, 2, 64), buf(2, 4, 2, 64), pltpu.VMEM((128, 256), F32),
            buf(2, 4, 64), buf(2, 4, 2, 64), buf(2, 64), buf(2, 2, 64), buf(2, 4, 64), buf(8, 64),
            buf(4, 4, 2, 64), buf(4, 4, 2, 32), buf(2, 4, 2, 2, 64), buf(2, 4, 2, 2, 32),
            buf(4, 32), buf(4, 32), buf(2, 4, 2, 32),
            pltpu.SemaphoreType.DMA((CHUNKS,)),
            pltpu.SemaphoreType.DMA((MESSAGES,)),
            pltpu.SemaphoreType.DMA((MESSAGES,)),
        ],
        compiler_params=pltpu.CompilerParams(
            collective_id=0, has_side_effects=True, vmem_limit_bytes=48 << 20
        ),
        name="tucker",
    )(fields, jnp.concatenate([factor_three.T, factor_two.T, factor_one.T], 1))
    return core.reshape(2, RANK, RANK, RANK), g1, g2


def solution(mesh):
    placed = (P(None, "row", "col", None), P("row", None), P("col", None), P())
    return jax.shard_map(
        body,
        mesh=mesh,
        in_specs=placed,
        out_specs=(P(), P(None, "row", "col"), P(None, "col", "row")),
        check_vma=False,
    )
```

```python
import functools

import jax
import jax.numpy as jnp
from jax import lax
from jax.experimental import pallas as pl
from jax.experimental.pallas import tpu as pltpu
from jax.sharding import PartitionSpec as P

F32 = jnp.float32
BF16 = jnp.bfloat16
MESH = pl.DeviceIdType.MESH
RANK = 32
CHUNKS = 4


def split(x):
    high = x.astype(BF16)
    return high, (x - high.astype(F32)).astype(BF16)


def dot(a, b, dims):
    return lax.dot_general(a, b, ((dims[0], dims[1]), ((), ())), preferred_element_type=F32)


def stack_factor(f):
    high, low = split(f)
    return jnp.concatenate([jnp.concatenate([high, high], 1), jnp.concatenate([low, low], 1)], 0)


def kernel(
    fields, factors, core_out, g1_out, g2_out,
    xbuf, p3, p2, p1, wcore,
    ry1, ryf, rz1, rzf, rc1, rc2,
    p2c, p1t, p2r, p1r, cy, cz, cc,
    xsem, ss, rs,
):
    r, c = lax.axis_index("row"), lax.axis_index("col")
    y, h = r // 4, r % 4
    l, x, co = c // 8, (c // 2) % 4, c % 2

    def ring(v, d):
        return (v + d) % 4

    def at_y(d):
        return (ring(y, d) * 4 + h, c)

    def at_h(d):
        return (y * 4 + ring(h, d), c)

    def at_x(d):
        return (r, l * 8 + ring(x, d) * 2 + co)

    at_l = (r, (1 - l) * 8 + x * 2 + co)
    at_co = (r, l * 8 + x * 2 + (1 - co))
    x_r = (r // 2) % 4
    at_t2 = (c, (h // 2) * 8 + ring(y, x) * 2 + h % 2)
    at_t1 = ((ring(x, 4 - x_r)) * 4 + l * 2 + co, r)
    away = jnp.logical_or(at_t2[0] != r, at_t2[1] != c)

    def load(i):
        return pltpu.make_async_copy(fields.at[i // 2, pl.ds(i % 2 * 32, 32)], xbuf.at[i], xsem.at[i])

    for i in range(CHUNKS):
        load(i).start()
    barrier = pltpu.get_barrier_semaphore()
    def at_lx(d):
        return (r, (1 - l) * 8 + ring(x, d) * 2 + co)

    partners = [at(d) for at in (at_y, at_h, at_x, at_lx) for d in (1, 2, 3)] + [at_l, at_co]
    for to in partners:
        pl.semaphore_signal(barrier, inc=1, device_id=to, device_id_type=MESH)

    @pl.when(away)
    def _():
        pl.semaphore_signal(barrier, inc=1, device_id=at_t1, device_id_type=MESH)
        pl.semaphore_signal(barrier, inc=1, device_id=at_t2, device_id_type=MESH)

    sent = []

    def copy(idx, src, dst, to):
        return pltpu.make_async_remote_copy(
            src_ref=src, dst_ref=dst, send_sem=ss.at[idx], recv_sem=rs.at[idx], device_id=to, device_id_type=MESH
        )

    counter = [0]

    def new(n=1):
        counter[0] += n
        return counter[0] - n

    def send(idx, src, dst, to):
        copy(idx, src, dst, to).start()
        sent.append((idx, src))

    def arrived(idx, dst):
        copy(idx, dst, dst, at_co).wait_recv()

    f3, f1, f2 = factors[:, :128], factors[:, 256:320], factors[:, 128:256]
    l3, l1, l2 = stack_factor(f3), stack_factor(f1), stack_factor(f2)
    wcore[...] = jnp.zeros_like(wcore)
    for b in range(4):
        wcore[pl.ds(b * 32, 32), pl.ds(b * 64, 64)] = f1

    def project(i, _):
        load(i).wait()
        for n in range(16):
            high, low = split(xbuf[i, pl.ds(n * 2, 2)].reshape(256, 128))
            out = dot(l3, jnp.concatenate([high, low], 1), ((1,), (1,)))
            out = out[:RANK] + out[RANK:]
            at = pl.multiple_of(i * 32 * RANK, RANK) + n * 2 * RANK
            p3[pl.ds(at, RANK), :] = out[:, :128]
            p3[pl.ds(at + RANK, RANK), :] = out[:, 128:]
        return 0

    lax.fori_loop(0, CHUNKS, project, 0)

    def mode_two(ys, hs):
        k = ys * 4 + hs
        right = []
        for half in range(2):
            hi, lo = split(p3[pl.ds(k + 16 * half, 128, stride=RANK), :])
            right.extend(jnp.concatenate([hi[s * 64:s * 64 + 64], lo[s * 64:s * 64 + 64]], 0) for s in range(2))
        out = dot(l1, jnp.concatenate(right, 1), ((1,), (0,)))
        out = out[:RANK] + out[RANK:]
        for half in range(2):
            for s in range(2):
                at = half * 256 + s * 128
                p2[ys, hs, s, pl.ds(half * RANK, RANK), :] = out[:, at:at + 128]

    def mode_one(k):
        parts = [jnp.concatenate(split(p3[pl.ds(half * 16 + k, 128, stride=RANK), :]), 1) for half in range(2)]
        out = dot(l2, jnp.concatenate(parts, 0), ((1,), (1,)))
        out = out[:RANK] + out[RANK:]
        for half in range(2):
            p1[k // 8, (k // 2) % 4, k % 2, pl.ds(half * RANK, RANK), :] = out[:, half * 128:half * 128 + 128]

    pl.semaphore_wait(barrier, len(partners) + jnp.where(away, 2, 0))

    order = (2, 1, 3, 0)
    m_y1 = [new(4), new(4)]
    m_yf = {(side, s): new(4) for side in range(2) for s in range(2)}

    m_core, m_x = new(), new(8)
    for k in range(16):
        mode_one(k)
    send(m_core, p1.at[:, :, 1 - co], rc1, at_co)
    for dy in order:
        if dy == 3:
            arrived(m_core, rc1)
            for lk in range(2):
                for xk in range(4):
                    p1[lk, xk, co] += rc1[lk, xk]
            for d in (2, 1, 3):
                send(m_x + d, p1.at[l, ring(x, d), co], rc2.at[d], at_x(d))
                send(m_x + 4 + d, p1.at[1 - l, ring(x, d), co], rc2.at[4 + d], at_lx(d))
            send(m_x + 4, p1.at[1 - l, x, co], rc2.at[4], at_l)
        for n, dh in enumerate(order):
            ys, hs = ring(y, dy), ring(h, dh)
            mode_two(ys, hs)
            if dy == 2:
                send(m_y1[0] + n, p2.at[ys, hs, 0], ry1.at[0, hs], at_y(1))
                send(m_y1[1] + n, p2.at[ys, hs, 1], ry1.at[1, hs], at_y(3))

    def y_late(n):
        hs = ring(h, order[n])
        up, down = ring(y, 1), ring(y, 3)
        send(m_yf[0, 1] + n, p2.at[up, hs, 1], ryf.at[0, hs, 1], at_y(1))
        send(m_yf[1, 0] + n, p2.at[down, hs, 0], ryf.at[1, hs, 0], at_y(3))
        arrived(m_y1[0] + n, ry1.at[0, hs])
        p2[up, hs, 0] += ry1[0, hs]
        send(m_yf[0, 0] + n, p2.at[up, hs, 0], ryf.at[0, hs, 0], at_y(1))
        arrived(m_y1[1] + n, ry1.at[1, hs])
        p2[down, hs, 1] += ry1[1, hs]
        send(m_yf[1, 1] + n, p2.at[down, hs, 1], ryf.at[1, hs, 1], at_y(3))

    def y_final(n):
        hs = ring(h, order[n])
        for s in (1, 0):
            for side in range(2):
                arrived(m_yf[side, s] + n, ryf.at[side, hs, s])
            p2[y, hs, s] += ryf[0, hs, s] + ryf[1, hs, s]

    def gather_row(buf):
        mz = new(6)
        my = [new(4) for _ in range(4)]

        def to_y(dh):
            mine = buf.at[y, ring(h, dh)]
            send(my[dh], mine, mine, at_y(1))
            send(my[dh] + 1, mine, mine, at_y(3))

        def y_step(dh):
            hs = ring(h, dh)
            got = buf.at[ring(y, 3), hs]
            arrived(my[dh], got)
            send(my[dh] + 2, got.at[0], got.at[0], at_y(1))
            got = buf.at[ring(y, 1), hs]
            arrived(my[dh] + 1, got)
            send(my[dh] + 3, got.at[1], got.at[1], at_y(3))

        mine = buf.at[y, h]
        for half in range(2):
            send(mz + 4 * half, mine.at[half], mine.at[half], at_h(1))
            send(mz + 1 + 4 * half, mine.at[1 - half], mine.at[1 - half], at_h(3))
        to_y(0)
        yield
        y_step(0)
        yield
        below, above = buf.at[y, ring(h, 3)], buf.at[y, ring(h, 1)]
        arrived(mz, below.at[0])
        send(mz + 2, below.at[0], below.at[0], at_h(1))
        arrived(mz + 1, above.at[1])
        send(mz + 3, above.at[1], above.at[1], at_h(3))
        arrived(mz + 4, below.at[1])
        to_y(3)
        arrived(mz + 5, above.at[0])
        to_y(1)
        yield
        got = buf.at[y, ring(h, 2)]
        arrived(mz + 2, got.at[0])
        arrived(mz + 3, got.at[1])
        to_y(2)
        yield
        y_step(3)
        y_step(1)
        yield
        y_step(2)
        yield
        for dh in (0, 3, 1, 2):
            got = buf.at[ring(y, 2), ring(h, dh)]
            arrived(my[dh] + 2, got.at[0])
            arrived(my[dh] + 3, got.at[1])
        yield

    def gather_col(buf):
        ml = new()
        mx = [new(4), new(4)]
        mc = new(8)

        def to_x(lk, k):
            mine = buf.at[lk, x, co]
            send(mx[k], mine, mine, at_x(1))
            send(mx[k] + 1, mine, mine, at_x(3))
            if k:
                send(mx[k] + 2, mine, mine, at_x(2))

        def to_co(lk, k, dx):
            mine = buf.at[lk, ring(x, dx), co]
            send(mc + k * 4 + dx, mine, mine, at_co)

        def x_step(lk, k):
            got = buf.at[lk, ring(x, 3), co]
            arrived(mx[k], got)
            if not k:
                send(mx[k] + 2, got.at[0], got.at[0], at_x(1))
            to_co(lk, k, 3)
            got = buf.at[lk, ring(x, 1), co]
            arrived(mx[k] + 1, got)
            if not k:
                send(mx[k] + 3, got.at[1], got.at[1], at_x(3))
            to_co(lk, k, 1)

        mine = buf.at[l, x, co]
        send(ml, mine, mine, at_l)
        to_x(l, 0)
        to_co(l, 0, 0)
        yield
        arrived(ml, buf.at[1 - l, x, co])
        to_x(1 - l, 1)
        to_co(1 - l, 1, 0)
        yield
        x_step(l, 0)
        yield
        x_step(1 - l, 1)
        yield
        for k, lk in enumerate((l, 1 - l)):
            got = buf.at[lk, ring(x, 2), co]
            if k:
                arrived(mx[k] + 2, got)
            else:
                arrived(mx[k] + 2, got.at[0])
                arrived(mx[k] + 3, got.at[1])
            to_co(lk, k, 2)
        yield
        for k, lk in enumerate((l, 1 - l)):
            for dx in range(4):
                arrived(mc + k * 4 + dx, buf.at[lk, ring(x, dx), 1 - co])
        yield

    for n in range(4):
        y_late(n)

    m_z1 = [new(), new()]
    m_zf = {(side, s): new() for side in range(2) for s in range(2)}
    y_final(0)
    send(m_z1[0], p2.at[y, ring(h, 2), 0], rz1.at[0], at_h(1))
    send(m_z1[1], p2.at[y, ring(h, 2), 1], rz1.at[1], at_h(3))
    piece = p1[l, x, co]
    for k in range(1, 8):
        arrived(m_x + k, rc2.at[k])
        piece = piece + rc2[k]
    p1r[l, x, co] = piece.reshape(2, RANK, 128)
    m_t1, m_t2 = new(), new()

    @pl.when(away)
    def _():
        copy(m_t1, p1r.at[l, x, co], p1t.at[ring(x, 4 - x_r), l * 2 + co], at_t1).start()

    @pl.when(jnp.logical_not(away))
    def _():
        p1t[y, h] = p1r[l, x, co]

    ag_p1r = gather_col(p1r)
    next(ag_p1r)
    wide = jnp.concatenate([piece[:RANK], piece[RANK:]], 1)
    cy[y] = lax.dot_general(wide, wcore[...], (((1,), (1,)), ((), ())), precision=lax.Precision.HIGHEST, preferred_element_type=F32)
    m_cy, m_cz, m_cx = new(3), new(3), new(3)
    for d in (2, 1, 3):
        send(m_cy + d - 1, cy.at[y], cy.at[y], at_y(d))

    y_final(1)
    send(m_zf[0, 1], p2.at[y, ring(h, 1), 1], rzf.at[0, 1], at_h(1))

    y_final(2)
    send(m_zf[1, 0], p2.at[y, ring(h, 3), 0], rzf.at[1, 0], at_h(3))
    arrived(m_z1[0], rz1.at[0])
    p2[y, ring(h, 1), 0] += rz1[0]
    send(m_zf[0, 0], p2.at[y, ring(h, 1), 0], rzf.at[0, 0], at_h(1))
    arrived(m_z1[1], rz1.at[1])
    p2[y, ring(h, 3), 1] += rz1[1]
    send(m_zf[1, 1], p2.at[y, ring(h, 3), 1], rzf.at[1, 1], at_h(3))
    y_final(3)
    next(ag_p1r)

    for d in (1, 2, 3):
        arrived(m_cy + d - 1, cy.at[ring(y, 4 - d)])
    cz[h] = cy[0] + cy[1] + cy[2] + cy[3]
    for d in (2, 1, 3):
        send(m_cz + d - 1, cz.at[h], cz.at[h], at_h(d))
    next(ag_p1r)

    for s in (1, 0):
        for side in range(2):
            arrived(m_zf[side, s], rzf.at[side, s])
        p2c[y, h, s] = p2[y, h, s] + rzf[0, s] + rzf[1, s]

    @pl.when(away)
    def _():
        copy(m_t2, p2c.at[y, h], p2r.at[h // 2, ring(y, x), h % 2], at_t2).start()

    @pl.when(jnp.logical_not(away))
    def _():
        p2r[l, x, co] = p2c[y, h]

    ag_p2c = gather_row(p2c)
    next(ag_p2c)

    @pl.when(away)
    def _():
        copy(m_t1, p1t.at[y, h], p1t.at[y, h], at_t2).wait_recv()

    ag_p1t = gather_row(p1t)
    next(ag_p1t)
    next(ag_p1r)
    for d in (1, 2, 3):
        arrived(m_cz + d - 1, cz.at[ring(h, 4 - d)])
    cc[l, x, co] = cz[0] + cz[1] + cz[2] + cz[3]
    for d in (2, 1, 3):
        send(m_cx + d - 1, cc.at[l, x, co], cc.at[l, x, co], at_x(d))
    next(ag_p1r)
    next(ag_p2c)
    @pl.when(away)
    def _():
        copy(m_t2, p2r.at[l, x, co], p2r.at[l, x, co], at_t2).wait_recv()

    ag_p2r = gather_col(p2r)
    next(ag_p2r)
    next(ag_p1t)

    next(ag_p2c)
    next(ag_p1t)
    for d in (1, 2, 3):
        arrived(m_cx + d - 1, cc.at[l, ring(x, 4 - d), co])
    m_cl, m_cc = new(), new()
    send(m_cl, cc.at[l, :, co], cc.at[l, :, co], at_l)
    next(ag_p1t)
    next(ag_p2r)
    next(ag_p2r)
    next(ag_p2c)
    next(ag_p2c)
    next(ag_p1t)
    arrived(m_cl, cc.at[1 - l, :, co])
    send(m_cc, cc.at[:, :, co], cc.at[:, :, co], at_co)
    next(ag_p2r)
    next(ag_p2c)
    next(ag_p1t)
    next(ag_p2r)
    scale = 1.0 / (RANK * RANK)

    def gram(a, b):
        ah, al = split(a.T)
        bh, bl = split(b)
        left = jnp.concatenate([ah, al], 0)
        out = dot(left, bh, ((1,), (0,)))
        return out[:128] + out[128:] + dot(ah, bl, ((1,), (0,)))

    next(ag_p1r)
    next(ag_p1t)
    g = sum(gram(p1r[:, ring(x, d)].reshape(256, 128), p1t[d].reshape(256, 128)) for d in range(4)) * scale
    g1_out[0] = g[:64, :64]
    g1_out[1] = g[64:, 64:]

    arrived(m_cc, cc.at[:, :, 1 - co])
    flat = cc.reshape(16 * RANK, 128)
    for q4 in range(8):
        rows = []
        for j in range(4):
            mine = flat[pl.ds(q4 * 4 + j, 16, stride=RANK), :]
            rows.extend((mine[:, :64], mine[:, 64:]))
        turned = jnp.concatenate(rows, 0).T
        core_out[pl.ds(q4, 64, stride=8), :] = turned
    next(ag_p2r)

    def partial(dy):
        ys = ring(y, dy)
        return [
            gram(
                p2c[ys, :, s].reshape(256, 128),
                p2r[:, ring(ys, x_r), :, s].reshape(256, 128),
            )
            for s in range(2)
        ]

    early = len(sent) - 12
    for idx, src in sent[:early]:
        copy(idx, src, src, at_co).wait_send()
    total = [partial(dy) for dy in (0, 1, 3)]
    next(ag_p2c)
    total.append(partial(2))
    for s in range(2):
        g2_out[s] = sum(t[s] for t in total) * scale

    for idx, src in sent[early:]:
        copy(idx, src, src, at_co).wait_send()

    @pl.when(away)
    def _():
        copy(m_t1, p1r.at[l, x, co], p1r.at[l, x, co], at_t2).wait_send()
        copy(m_t2, p2c.at[y, h], p2c.at[y, h], at_t2).wait_send()

    assert counter[0] <= MESSAGES, counter[0]


MESSAGES = 160


def body(fields, factor_one, factor_two, factor_three):
    vmem = pl.BlockSpec(memory_space=pltpu.VMEM)

    def buf(*shape):
        return pltpu.VMEM((*shape, 128), F32)

    core, g1, g2 = pl.pallas_call(
        kernel,
        out_shape=(
            jax.ShapeDtypeStruct((512, 128), F32),
            jax.ShapeDtypeStruct((2, 64, 64), F32),
            jax.ShapeDtypeStruct((2, 128, 128), F32),
        ),
        in_specs=[pl.BlockSpec(memory_space=pl.ANY), vmem],
        out_specs=(vmem, vmem, vmem),
        scratch_shapes=[
            buf(CHUNKS, 32, 128), buf(4096), buf(4, 4, 2, 64), buf(2, 4, 2, 64), pltpu.VMEM((128, 256), F32),
            buf(2, 4, 64), buf(2, 4, 2, 64), buf(2, 64), buf(2, 2, 64), buf(2, 4, 64), buf(8, 64),
            buf(4, 4, 2, 64), buf(4, 4, 2, 32), buf(2, 4, 2, 2, 64), buf(2, 4, 2, 2, 32),
            buf(4, 32), buf(4, 32), buf(2, 4, 2, 32),
            pltpu.SemaphoreType.DMA((CHUNKS,)),
            pltpu.SemaphoreType.DMA((MESSAGES,)),
            pltpu.SemaphoreType.DMA((MESSAGES,)),
        ],
        compiler_params=pltpu.CompilerParams(
            collective_id=0, has_side_effects=True, vmem_limit_bytes=48 << 20
        ),
        name="tucker",
    )(fields, jnp.concatenate([factor_three.T, factor_two.T, factor_one.T], 1))
    return core.reshape(2, RANK, RANK, RANK), g1, g2


def solution(mesh):
    placed = (P(None, "row", "col", None), P("row", None), P("col", None), P())
    return jax.shard_map(
        body,
        mesh=mesh,
        in_specs=placed,
        out_specs=(P(), P(None, "row", "col"), P(None, "col", "row")),
        check_vma=False,
    )
```

```python
import functools

import jax
import jax.numpy as jnp
from jax import lax
from jax.experimental import pallas as pl
from jax.experimental.pallas import tpu as pltpu
from jax.sharding import PartitionSpec as P

F32 = jnp.float32
BF16 = jnp.bfloat16
MESH = pl.DeviceIdType.MESH
RANK = 32
CHUNKS = 4


def split(x):
    high = x.astype(BF16)
    return high, (x - high.astype(F32)).astype(BF16)


def dot(a, b, dims):
    return lax.dot_general(a, b, ((dims[0], dims[1]), ((), ())), preferred_element_type=F32)


def stack_factor(f):
    high, low = split(f)
    return jnp.concatenate([jnp.concatenate([high, high], 1), jnp.concatenate([low, low], 1)], 0)


def kernel(
    fields, factors, core_out, g1_out, g2_out,
    xbuf, p3, p2, p1, wcore,
    ry1, ryf, rz1, rzf, rc1, rc2,
    p2c, p1t, p2r, p1r, cy, cz, cc,
    xsem, ss, rs,
):
    r, c = lax.axis_index("row"), lax.axis_index("col")
    y, h = r // 4, r % 4
    l, x, co = c // 8, (c // 2) % 4, c % 2

    def ring(v, d):
        return (v + d) % 4

    def at_y(d):
        return (ring(y, d) * 4 + h, c)

    def at_h(d):
        return (y * 4 + ring(h, d), c)

    def at_x(d):
        return (r, l * 8 + ring(x, d) * 2 + co)

    at_l = (r, (1 - l) * 8 + x * 2 + co)
    at_co = (r, l * 8 + x * 2 + (1 - co))
    x_r = (r // 2) % 4
    at_t2 = (c, (h // 2) * 8 + ring(y, x) * 2 + h % 2)
    at_t1 = ((ring(x, 4 - x_r)) * 4 + l * 2 + co, r)
    away = jnp.logical_or(at_t2[0] != r, at_t2[1] != c)

    def load(i):
        return pltpu.make_async_copy(fields.at[i // 2, pl.ds(i % 2 * 32, 32)], xbuf.at[i], xsem.at[i])

    for i in range(CHUNKS):
        load(i).start()
    barrier = pltpu.get_barrier_semaphore()
    def at_lx(d):
        return (r, (1 - l) * 8 + ring(x, d) * 2 + co)

    partners = [at(d) for at in (at_y, at_h, at_x, at_lx) for d in (1, 2, 3)] + [at_l, at_co]
    for to in partners:
        pl.semaphore_signal(barrier, inc=1, device_id=to, device_id_type=MESH)

    @pl.when(away)
    def _():
        pl.semaphore_signal(barrier, inc=1, device_id=at_t1, device_id_type=MESH)
        pl.semaphore_signal(barrier, inc=1, device_id=at_t2, device_id_type=MESH)

    sent = []

    def copy(idx, src, dst, to):
        return pltpu.make_async_remote_copy(
            src_ref=src, dst_ref=dst, send_sem=ss.at[idx], recv_sem=rs.at[idx], device_id=to, device_id_type=MESH
        )

    counter = [0]

    def new(n=1):
        counter[0] += n
        return counter[0] - n

    def send(idx, src, dst, to):
        copy(idx, src, dst, to).start()
        sent.append((idx, src))

    def arrived(idx, dst):
        copy(idx, dst, dst, at_co).wait_recv()

    f3, f1, f2 = factors[:, :128], factors[:, 256:320], factors[:, 128:256]
    l3, l1, l2 = stack_factor(f3), stack_factor(f1), stack_factor(f2)
    wcore[...] = jnp.zeros_like(wcore)
    for b in range(4):
        wcore[pl.ds(b * 32, 32), pl.ds(b * 64, 64)] = f1

    def project(i, _):
        load(i).wait()
        for n in range(16):
            high, low = split(xbuf[i, pl.ds(n * 2, 2)].reshape(256, 128))
            out = dot(l3, jnp.concatenate([high, low], 1), ((1,), (1,)))
            out = out[:RANK] + out[RANK:]
            at = pl.multiple_of(i * 32 * RANK, RANK) + n * 2 * RANK
            p3[pl.ds(at, RANK), :] = out[:, :128]
            p3[pl.ds(at + RANK, RANK), :] = out[:, 128:]
        return 0

    lax.fori_loop(0, CHUNKS, project, 0)

    def mode_two(ys, hs):
        k = ys * 4 + hs
        right = []
        for half in range(2):
            hi, lo = split(p3[pl.ds(k + 16 * half, 128, stride=RANK), :])
            right.extend(jnp.concatenate([hi[s * 64:s * 64 + 64], lo[s * 64:s * 64 + 64]], 0) for s in range(2))
        out = dot(l1, jnp.concatenate(right, 1), ((1,), (0,)))
        out = out[:RANK] + out[RANK:]
        for half in range(2):
            for s in range(2):
                at = half * 256 + s * 128
                p2[ys, hs, s, pl.ds(half * RANK, RANK), :] = out[:, at:at + 128]

    def mode_one(k):
        parts = [jnp.concatenate(split(p3[pl.ds(half * 16 + k, 128, stride=RANK), :]), 1) for half in range(2)]
        out = dot(l2, jnp.concatenate(parts, 0), ((1,), (1,)))
        out = out[:RANK] + out[RANK:]
        for half in range(2):
            p1[k // 8, (k // 2) % 4, k % 2, pl.ds(half * RANK, RANK), :] = out[:, half * 128:half * 128 + 128]

    pl.semaphore_wait(barrier, len(partners) + jnp.where(away, 2, 0))

    order = (2, 1, 3, 0)
    m_y1 = [new(4), new(4)]
    m_yf = {(side, s): new(4) for side in range(2) for s in range(2)}

    m_core, m_x = new(), new(8)
    for k in range(16):
        mode_one(k)
    send(m_core, p1.at[:, :, 1 - co], rc1, at_co)
    for dy in order:
        if dy == 3:
            arrived(m_core, rc1)
            for lk in range(2):
                for xk in range(4):
                    p1[lk, xk, co] += rc1[lk, xk]
            for d in (2, 1, 3):
                send(m_x + d, p1.at[l, ring(x, d), co], rc2.at[d], at_x(d))
                send(m_x + 4 + d, p1.at[1 - l, ring(x, d), co], rc2.at[4 + d], at_lx(d))
            send(m_x + 4, p1.at[1 - l, x, co], rc2.at[4], at_l)
        for n, dh in enumerate(order):
            ys, hs = ring(y, dy), ring(h, dh)
            mode_two(ys, hs)
            if dy == 2:
                send(m_y1[0] + n, p2.at[ys, hs, 0], ry1.at[0, hs], at_y(1))
                send(m_y1[1] + n, p2.at[ys, hs, 1], ry1.at[1, hs], at_y(3))

    def y_late(n):
        hs = ring(h, order[n])
        up, down = ring(y, 1), ring(y, 3)
        send(m_yf[0, 1] + n, p2.at[up, hs, 1], ryf.at[0, hs, 1], at_y(1))
        send(m_yf[1, 0] + n, p2.at[down, hs, 0], ryf.at[1, hs, 0], at_y(3))
        arrived(m_y1[0] + n, ry1.at[0, hs])
        p2[up, hs, 0] += ry1[0, hs]
        send(m_yf[0, 0] + n, p2.at[up, hs, 0], ryf.at[0, hs, 0], at_y(1))
        arrived(m_y1[1] + n, ry1.at[1, hs])
        p2[down, hs, 1] += ry1[1, hs]
        send(m_yf[1, 1] + n, p2.at[down, hs, 1], ryf.at[1, hs, 1], at_y(3))

    def y_final(n):
        hs = ring(h, order[n])
        for s in (1, 0):
            for side in range(2):
                arrived(m_yf[side, s] + n, ryf.at[side, hs, s])
            p2[y, hs, s] += ryf[0, hs, s] + ryf[1, hs, s]

    def gather_row(buf):
        mz = new(6)
        my = [new(4) for _ in range(4)]

        def to_y(dh):
            mine = buf.at[y, ring(h, dh)]
            send(my[dh], mine, mine, at_y(1))
            send(my[dh] + 1, mine, mine, at_y(3))

        def y_step(dh):
            hs = ring(h, dh)
            got = buf.at[ring(y, 3), hs]
            arrived(my[dh], got)
            send(my[dh] + 2, got.at[0], got.at[0], at_y(1))
            got = buf.at[ring(y, 1), hs]
            arrived(my[dh] + 1, got)
            send(my[dh] + 3, got.at[1], got.at[1], at_y(3))

        mine = buf.at[y, h]
        for half in range(2):
            send(mz + 4 * half, mine.at[half], mine.at[half], at_h(1))
            send(mz + 1 + 4 * half, mine.at[1 - half], mine.at[1 - half], at_h(3))
        to_y(0)
        yield
        y_step(0)
        yield
        below, above = buf.at[y, ring(h, 3)], buf.at[y, ring(h, 1)]
        arrived(mz, below.at[0])
        send(mz + 2, below.at[0], below.at[0], at_h(1))
        arrived(mz + 1, above.at[1])
        send(mz + 3, above.at[1], above.at[1], at_h(3))
        arrived(mz + 4, below.at[1])
        to_y(3)
        arrived(mz + 5, above.at[0])
        to_y(1)
        yield
        got = buf.at[y, ring(h, 2)]
        arrived(mz + 2, got.at[0])
        arrived(mz + 3, got.at[1])
        to_y(2)
        yield
        y_step(3)
        y_step(1)
        yield
        y_step(2)
        yield
        for dh in (0, 3, 1, 2):
            got = buf.at[ring(y, 2), ring(h, dh)]
            arrived(my[dh] + 2, got.at[0])
            arrived(my[dh] + 3, got.at[1])
        yield

    def gather_col(buf, direct=(False, True)):
        ml = new()
        mx = [new(4), new(4)]
        mc = new(8)

        def to_x(lk, k):
            mine = buf.at[lk, x, co]
            send(mx[k], mine, mine, at_x(1))
            send(mx[k] + 1, mine, mine, at_x(3))
            if direct[k]:
                send(mx[k] + 2, mine, mine, at_x(2))

        def to_co(lk, k, dx):
            mine = buf.at[lk, ring(x, dx), co]
            send(mc + k * 4 + dx, mine, mine, at_co)

        def x_step(lk, k):
            got = buf.at[lk, ring(x, 3), co]
            arrived(mx[k], got)
            if not direct[k]:
                send(mx[k] + 2, got.at[0], got.at[0], at_x(1))
            to_co(lk, k, 3)
            got = buf.at[lk, ring(x, 1), co]
            arrived(mx[k] + 1, got)
            if not direct[k]:
                send(mx[k] + 3, got.at[1], got.at[1], at_x(3))
            to_co(lk, k, 1)

        mine = buf.at[l, x, co]
        send(ml, mine, mine, at_l)
        to_x(l, 0)
        to_co(l, 0, 0)
        yield
        arrived(ml, buf.at[1 - l, x, co])
        to_x(1 - l, 1)
        to_co(1 - l, 1, 0)
        yield
        x_step(l, 0)
        yield
        x_step(1 - l, 1)
        yield
        for k, lk in enumerate((l, 1 - l)):
            got = buf.at[lk, ring(x, 2), co]
            if direct[k]:
                arrived(mx[k] + 2, got)
            else:
                arrived(mx[k] + 2, got.at[0])
                arrived(mx[k] + 3, got.at[1])
            to_co(lk, k, 2)
        yield
        for k, lk in enumerate((l, 1 - l)):
            for dx in range(4):
                arrived(mc + k * 4 + dx, buf.at[lk, ring(x, dx), 1 - co])
        yield

    for n in range(4):
        y_late(n)

    m_z1 = [new(), new()]
    m_zf = {(side, s): new() for side in range(2) for s in range(2)}
    y_final(0)
    send(m_z1[0], p2.at[y, ring(h, 2), 0], rz1.at[0], at_h(1))
    send(m_z1[1], p2.at[y, ring(h, 2), 1], rz1.at[1], at_h(3))
    piece = p1[l, x, co]
    for k in range(1, 8):
        arrived(m_x + k, rc2.at[k])
        piece = piece + rc2[k]
    p1r[l, x, co] = piece.reshape(2, RANK, 128)
    m_t1, m_t2 = new(), new()

    @pl.when(away)
    def _():
        copy(m_t1, p1r.at[l, x, co], p1t.at[ring(x, 4 - x_r), l * 2 + co], at_t1).start()

    @pl.when(jnp.logical_not(away))
    def _():
        p1t[y, h] = p1r[l, x, co]

    ag_p1r = gather_col(p1r, (False, False))
    next(ag_p1r)
    wide = jnp.concatenate([piece[:RANK], piece[RANK:]], 1)
    cy[y] = lax.dot_general(wide, wcore[...], (((1,), (1,)), ((), ())), precision=lax.Precision.HIGHEST, preferred_element_type=F32)
    m_cy, m_cz, m_cx = new(3), new(3), new(3)
    for d in (2, 1, 3):
        send(m_cy + d - 1, cy.at[y], cy.at[y], at_y(d))

    y_final(1)
    send(m_zf[0, 1], p2.at[y, ring(h, 1), 1], rzf.at[0, 1], at_h(1))

    y_final(2)
    send(m_zf[1, 0], p2.at[y, ring(h, 3), 0], rzf.at[1, 0], at_h(3))
    arrived(m_z1[0], rz1.at[0])
    p2[y, ring(h, 1), 0] += rz1[0]
    send(m_zf[0, 0], p2.at[y, ring(h, 1), 0], rzf.at[0, 0], at_h(1))
    arrived(m_z1[1], rz1.at[1])
    p2[y, ring(h, 3), 1] += rz1[1]
    send(m_zf[1, 1], p2.at[y, ring(h, 3), 1], rzf.at[1, 1], at_h(3))
    y_final(3)
    next(ag_p1r)

    for d in (1, 2, 3):
        arrived(m_cy + d - 1, cy.at[ring(y, 4 - d)])
    cz[h] = cy[0] + cy[1] + cy[2] + cy[3]
    for d in (2, 1, 3):
        send(m_cz + d - 1, cz.at[h], cz.at[h], at_h(d))
    next(ag_p1r)

    for s in (1, 0):
        for side in range(2):
            arrived(m_zf[side, s], rzf.at[side, s])
        p2c[y, h, s] = p2[y, h, s] + rzf[0, s] + rzf[1, s]

    @pl.when(away)
    def _():
        copy(m_t2, p2c.at[y, h], p2r.at[h // 2, ring(y, x), h % 2], at_t2).start()

    @pl.when(jnp.logical_not(away))
    def _():
        p2r[l, x, co] = p2c[y, h]

    ag_p2c = gather_row(p2c)
    next(ag_p2c)

    @pl.when(away)
    def _():
        copy(m_t1, p1t.at[y, h], p1t.at[y, h], at_t2).wait_recv()

    ag_p1t = gather_row(p1t)
    next(ag_p1t)
    next(ag_p1r)
    for d in (1, 2, 3):
        arrived(m_cz + d - 1, cz.at[ring(h, 4 - d)])
    cc[l, x, co] = cz[0] + cz[1] + cz[2] + cz[3]
    for d in (2, 1, 3):
        send(m_cx + d - 1, cc.at[l, x, co], cc.at[l, x, co], at_x(d))
    next(ag_p1r)
    next(ag_p2c)
    @pl.when(away)
    def _():
        copy(m_t2, p2r.at[l, x, co], p2r.at[l, x, co], at_t2).wait_recv()

    ag_p2r = gather_col(p2r)
    next(ag_p2r)
    next(ag_p1t)

    next(ag_p2c)
    next(ag_p1t)
    for d in (1, 2, 3):
        arrived(m_cx + d - 1, cc.at[l, ring(x, 4 - d), co])
    m_cl, m_cc = new(), new()
    send(m_cl, cc.at[l, :, co], cc.at[l, :, co], at_l)
    next(ag_p1t)
    next(ag_p2r)
    next(ag_p2r)
    next(ag_p2c)
    next(ag_p2c)
    next(ag_p1t)
    arrived(m_cl, cc.at[1 - l, :, co])
    send(m_cc, cc.at[:, :, co], cc.at[:, :, co], at_co)
    next(ag_p2r)
    next(ag_p2c)
    next(ag_p1t)
    next(ag_p2r)
    scale = 1.0 / (RANK * RANK)

    def gram(a, b):
        ah, al = split(a.T)
        bh, bl = split(b)
        left = jnp.concatenate([ah, al], 0)
        out = dot(left, bh, ((1,), (0,)))
        return out[:128] + out[128:] + dot(ah, bl, ((1,), (0,)))

    next(ag_p1r)
    next(ag_p1t)
    g = sum(gram(p1r[:, ring(x, d)].reshape(256, 128), p1t[d].reshape(256, 128)) for d in range(4)) * scale
    g1_out[0] = g[:64, :64]
    g1_out[1] = g[64:, 64:]

    arrived(m_cc, cc.at[:, :, 1 - co])
    flat = cc.reshape(16 * RANK, 128)
    for q4 in range(8):
        rows = []
        for j in range(4):
            mine = flat[pl.ds(q4 * 4 + j, 16, stride=RANK), :]
            rows.extend((mine[:, :64], mine[:, 64:]))
        turned = jnp.concatenate(rows, 0).T
        core_out[pl.ds(q4, 64, stride=8), :] = turned
    next(ag_p2r)

    def partial(dy):
        ys = ring(y, dy)
        return [
            gram(
                p2c[ys, :, s].reshape(256, 128),
                p2r[:, ring(ys, x_r), :, s].reshape(256, 128),
            )
            for s in range(2)
        ]

    early = len(sent) - 12
    for idx, src in sent[:early]:
        copy(idx, src, src, at_co).wait_send()
    total = [partial(dy) for dy in (0, 1, 3)]
    next(ag_p2c)
    total.append(partial(2))
    for s in range(2):
        g2_out[s] = sum(t[s] for t in total) * scale

    for idx, src in sent[early:]:
        copy(idx, src, src, at_co).wait_send()

    @pl.when(away)
    def _():
        copy(m_t1, p1r.at[l, x, co], p1r.at[l, x, co], at_t2).wait_send()
        copy(m_t2, p2c.at[y, h], p2c.at[y, h], at_t2).wait_send()

    assert counter[0] <= MESSAGES, counter[0]


MESSAGES = 160


def body(fields, factor_one, factor_two, factor_three):
    vmem = pl.BlockSpec(memory_space=pltpu.VMEM)

    def buf(*shape):
        return pltpu.VMEM((*shape, 128), F32)

    core, g1, g2 = pl.pallas_call(
        kernel,
        out_shape=(
            jax.ShapeDtypeStruct((512, 128), F32),
            jax.ShapeDtypeStruct((2, 64, 64), F32),
            jax.ShapeDtypeStruct((2, 128, 128), F32),
        ),
        in_specs=[pl.BlockSpec(memory_space=pl.ANY), vmem],
        out_specs=(vmem, vmem, vmem),
        scratch_shapes=[
            buf(CHUNKS, 32, 128), buf(4096), buf(4, 4, 2, 64), buf(2, 4, 2, 64), pltpu.VMEM((128, 256), F32),
            buf(2, 4, 64), buf(2, 4, 2, 64), buf(2, 64), buf(2, 2, 64), buf(2, 4, 64), buf(8, 64),
            buf(4, 4, 2, 64), buf(4, 4, 2, 32), buf(2, 4, 2, 2, 64), buf(2, 4, 2, 2, 32),
            buf(4, 32), buf(4, 32), buf(2, 4, 2, 32),
            pltpu.SemaphoreType.DMA((CHUNKS,)),
            pltpu.SemaphoreType.DMA((MESSAGES,)),
            pltpu.SemaphoreType.DMA((MESSAGES,)),
        ],
        compiler_params=pltpu.CompilerParams(
            collective_id=0, has_side_effects=True, vmem_limit_bytes=48 << 20
        ),
        name="tucker",
    )(fields, jnp.concatenate([factor_three.T, factor_two.T, factor_one.T], 1))
    return core.reshape(2, RANK, RANK, RANK), g1, g2


def solution(mesh):
    placed = (P(None, "row", "col", None), P("row", None), P("col", None), P())
    return jax.shard_map(
        body,
        mesh=mesh,
        in_specs=placed,
        out_specs=(P(), P(None, "row", "col"), P(None, "col", "row")),
        check_vma=False,
    )
```
